32 devices in a mesh: section: 2 (over x), dp: 4 (over z), expert: 4 (over y, core).
Axes of the slice: x: 2, y: 2, z: 4, core: 2. Of those that a mesh axis runs over, the one named last changes fastest.
Arguments:
- tokens: bfloat16 [2, 4096, 3584], P('section', ('dp', 'expert')), may hold values from -0.75 to 0.75
- routes: int32 [2, 4096, 2], P('section', ('dp', 'expert')), may hold values from 0 to 3, all different within a row; in each aligned block of 256 rows (0 to 255, 256 to 511, ..., all dimensions but the last counted through in order) at most 160 rows name the same one
- hidden_grad: bfloat16 [2, 4, 4, 640, 1024], P('section', 'dp', 'expert'), may hold values from -1.5 to 1.5
- w_gate: bfloat16 [2, 4, 3584, 1024], P('section', 'expert'), may hold values from -0.75 to 0.75
- w_up: bfloat16 [2, 4, 3584, 1024], P('section', 'expert'), may hold values from -0.75 to 0.75
Outputs:
- passed_grad: bfloat16 [2, 4096, 3584], P('section', ('dp', 'expert'))
- grad_gate: bfloat16 [2, 4, 3584, 1024], P('section', 'expert', 'dp')
- grad_up: bfloat16 [2, 4, 3584, 1024], P('section', 'expert', 'dp')
The draws below stay inside these ranges and needn't reach their ends.
Inputs may be any that keep to these rules, and one draw needn't show every extreme that they name: `routes`: each token names 2 different experts. Among the 256 tokens of one device at most 160 name the same expert, and in every draw some device's tokens name some expert exactly 160 times.
All inputs are finite; a program needn't handle non-finite values.
Results may differ from the reference program's by a relative error of at most 0.019.
Values may be sent and summed in bfloat16 or wider, within the bound.
No kernel may reach another device: no remote copies, remote signals or barrier semaphores. Data moves between devices by JAX's collectives and lax.ppermute only.
A program may use at most 192 MiB of HBM per device.

```python
import math
import jax
import jax.numpy as jnp
import numpy as np

D = 3584
FF = 1024
TOP = 2
TOK_DEV = 256
EXPERTS = 4
CAP = 160
SLOTS = 640
TOKENS = 4096
N_SECTION = 2
N_DP = 4
N_EXPERT = 4


def steps_of(rng, extent, cuts, least, largest):
    gain, own = 1.0, jax.random.fold_in(rng, 6)
    for position, shards_of in cuts:
        steps = jnp.exp(jax.random.uniform(jax.random.fold_in(own, position), (shards_of,), jnp.float32, least / len(cuts), largest / len(cuts)))
        gain = gain * jnp.repeat(steps, extent[position] // shards_of).reshape([-1 if axis == position else 1 for axis in range(len(extent))])
    return gain


def deal_out(own_key, own, number, rows, number_of, top, most, slope):
    sequence = jax.random.permutation(own_key, number_of)
    heavy_load, usual = load_shares(number_of, rows * top, most, slope, True), load_shares(number_of, rows * top, most, slope, False)
    places = jnp.arange(number_of)

    def named(lengths, offset_by):
        used = int((lengths > 0).sum())
        fixed = max(1, used // 4)
        shifted = fixed + (places - fixed + offset_by * (used - fixed)) % max(1, number_of - fixed)
        return jnp.zeros((number_of,), jnp.int32).at[sequence[jnp.where(places < fixed, places, shifted)]].set(jnp.asarray(lengths, jnp.int32))

    lengths = jnp.where(number % 4 == 0, named(heavy_load, number // 4), named(usual, number - number // 4 - 1))
    mixed = jax.random.permutation(jax.random.fold_in(own, 3), number_of)
    giver, taker = mixed[0:number_of // 2 * 2:2], mixed[1:number_of // 2 * 2:2]
    room = jnp.minimum(lengths[giver] - 1, most - lengths[taker]) // 2
    room = jnp.where((giver == sequence[0]) | (taker == sequence[0]) | (lengths[taker] == 0), 0, jnp.maximum(room, 0))
    shifted = jax.random.randint(jax.random.fold_in(own, 4), (number_of // 2,), 0, 1 << 20) % (room + 1)
    lengths = lengths.at[giver].add(-shifted).at[taker].add(shifted)
    labels = jnp.searchsorted(jnp.cumsum(lengths), jnp.arange(rows * top), side="right").astype(jnp.int32)
    grid = labels.reshape(top, rows).T
    grid = grid[jax.random.permutation(jax.random.fold_in(own, 1), rows)]
    offset_by = jax.random.randint(jax.random.fold_in(own, 2), (rows, 1), 0, top)
    return jnp.take_along_axis(grid, (jnp.arange(top)[None, :] + offset_by) % top, axis=1)


def load_shares(amount, total, limit, slope, full):
    portions = [(1 << 20) // math.isqrt(rank ** slope) + 1 for rank in range(1, amount + 1)]
    largest = limit if full else min(limit, max(-(-total // amount), total * portions[0] // sum(portions)))
    least = 1 if total - largest >= amount - 1 else 0
    holding, surplus = [largest] + [least] * (amount - 1), total - largest - least * (amount - 1)
    while surplus > 0:
        candidates = [i for i in range(1, amount) if holding[i] < largest] or [i for i in range(1, amount) if holding[i] < limit]
        pool, remaining = sum([portions[i] for i in candidates]), surplus
        for i in candidates:
            extra = min(limit - holding[i], max(1, remaining * portions[i] // pool), surplus)
            holding[i] = holding[i] + extra
            surplus = surplus - extra
    return np.array(holding)


def scatter_about(own_key, shape, deviation, most, pieces=(), kind=jnp.bfloat16):
    loudness = steps_of(own_key, shape, pieces, -0.22, 0.18) if pieces else 1.0
    result = jax.random.normal(own_key, shape, jnp.float32) * deviation * loudness
    return jnp.minimum(jnp.maximum(result, -most), most).astype(kind)


def setup_inputs(seed: int = 0) -> dict:
    arg_keys = jax.random.split(jax.random.key(seed), 6)
    tokens = scatter_about(arg_keys[0], (N_SECTION, TOKENS, D), 0.125, 0.75, ((0, 2), (1, 16)))
    routes_keys = jax.random.split(jax.random.fold_in(arg_keys[1], 1), N_SECTION * TOKENS // TOK_DEV)
    routes_turns = jax.random.permutation(jax.random.fold_in(arg_keys[1], 3), N_SECTION * TOKENS // TOK_DEV)
    routes = jax.vmap(lambda own, number: deal_out(jax.random.fold_in(arg_keys[1], 2), own, number, TOK_DEV, EXPERTS, TOP, CAP, 1))(routes_keys, routes_turns).reshape((N_SECTION, TOKENS, TOP))
    hidden_grad = scatter_about(arg_keys[2], (N_SECTION, N_DP, EXPERTS, SLOTS, FF), 0.25, 1.5, ((0, 2), (1, 4), (2, 4)))
    w_gate = scatter_about(arg_keys[3], (N_SECTION, EXPERTS, D, FF), (D // 64) ** -0.5, 0.75, ((0, 2), (1, 4)))
    w_up = scatter_about(arg_keys[4], (N_SECTION, EXPERTS, D, FF), (D // 64) ** -0.5, 0.75, ((0, 2), (1, 4)))
    return {"tokens": tokens, "routes": routes, "hidden_grad": hidden_grad, "w_gate": w_gate, "w_up": w_up}


def slot_numbers(route_rows, experts, capacity):
    marked = (route_rows[:, :, None] == jnp.arange(experts, dtype=jnp.int32)[None, None, :]).astype(jnp.int32)
    per_token = jnp.sum(marked, axis=1).astype(jnp.int32)
    earlier = (jnp.cumsum(per_token, axis=0) - per_token).astype(jnp.int32)
    within = jnp.sum(marked * earlier[:, None, :], axis=2).astype(jnp.int32)
    return (route_rows * capacity + within).astype(jnp.int32)


def sender_rows(token_rows, slots, slot_total):
    token_count = token_rows.shape[0]
    top_slots = slots.shape[1]
    owner = jnp.full((slot_total,), token_count, jnp.int32)
    owner = owner.at[slots.reshape(-1)].set(jnp.repeat(jnp.arange(token_count, dtype=jnp.int32), top_slots))
    padded = jnp.concatenate([token_rows, jnp.zeros((1, token_rows.shape[1]), token_rows.dtype)], axis=0)
    return padded[owner]


def swiglu_grads(grad_hidden, gate_pre, up_pre):
    sigmoid_gate = jax.nn.sigmoid(gate_pre)
    grad_gate_pre = grad_hidden * up_pre * sigmoid_gate * (1.0 + gate_pre * (1.0 - sigmoid_gate))
    grad_up_pre = grad_hidden * gate_pre * sigmoid_gate
    return grad_gate_pre.astype(jnp.bfloat16), grad_up_pre.astype(jnp.bfloat16)


def reference(tokens, routes, hidden_grad, w_gate, w_up):
    experts = EXPERTS
    capacity = CAP
    slot_total = SLOTS
    section_grads = []
    gate_out = []
    up_out = []
    for section_index in range(N_SECTION):
        gate_sums = [jnp.zeros((D, FF), jnp.float32) for expert_index in range(experts)]
        up_sums = [jnp.zeros((D, FF), jnp.float32) for expert_index in range(experts)]
        token_parts = []
        for group_index in range(N_DP):
            base = group_index * N_EXPERT * TOK_DEV
            slot_lists = []
            outgoing = []
            for source in range(N_EXPERT):
                first = base + source * TOK_DEV
                token_rows = tokens[section_index, first:first + TOK_DEV]
                slots = slot_numbers(routes[section_index, first:first + TOK_DEV], experts, capacity)
                slot_lists.append(slots)
                outgoing.append(sender_rows(token_rows, slots, slot_total).reshape(experts, capacity, D))
            returned_parts = []
            for expert_index in range(experts):
                received = jnp.concatenate([outgoing[source][expert_index] for source in range(N_EXPERT)], axis=0)
                gate_w = w_gate[section_index, expert_index]
                up_w = w_up[section_index, expert_index]
                gate_pre = jnp.dot(received, gate_w, preferred_element_type=jnp.float32)
                up_pre = jnp.dot(received, up_w, preferred_element_type=jnp.float32)
                grad_hidden = hidden_grad[section_index, group_index, expert_index].astype(jnp.float32)
                grad_gate_pre, grad_up_pre = swiglu_grads(grad_hidden, gate_pre, up_pre)
                slot_grad = (jnp.dot(grad_gate_pre, gate_w.T, preferred_element_type=jnp.float32)
                             + jnp.dot(grad_up_pre, up_w.T, preferred_element_type=jnp.float32)).astype(jnp.bfloat16)
                returned_parts.append(slot_grad.reshape(N_EXPERT, capacity, D))
                gate_sums[expert_index] = gate_sums[expert_index] + jnp.dot(received.T, grad_gate_pre, preferred_element_type=jnp.float32)
                up_sums[expert_index] = up_sums[expert_index] + jnp.dot(received.T, grad_up_pre, preferred_element_type=jnp.float32)
            for source in range(N_EXPERT):
                returned = jnp.concatenate([returned_parts[expert_index][source] for expert_index in range(experts)], axis=0)
                picked = returned[slot_lists[source]].astype(jnp.float32)
                token_parts.append(jnp.sum(picked, axis=1).astype(jnp.bfloat16))
        section_grads.append(jnp.concatenate(token_parts, axis=0))
        gate_out.append(jnp.stack([total.astype(jnp.bfloat16) for total in gate_sums], axis=0))
        up_out.append(jnp.stack([total.astype(jnp.bfloat16) for total in up_sums], axis=0))
    token_grad = jnp.stack(section_grads, axis=0)
    passed_grad = jnp.roll(token_grad, -1, axis=0)
    return passed_grad, jnp.stack(gate_out, axis=0), jnp.stack(up_out, axis=0)
```

```python
import jax
import jax.numpy as jnp
from jax import lax
from jax.experimental import pallas as pl
from jax.experimental.pallas import tpu as pltpu
from jax.sharding import PartitionSpec as P

BF16 = jnp.bfloat16
F32 = jnp.float32
VMEM_LIMIT = 56 * 1024 * 1024


def dot(a, b, contract=((1,), (0,))):
    return lax.dot_general(a, b, (contract, ((), ())), preferred_element_type=F32)


def grouped_pairs(count):
    first, last = 0, count - 1
    sets = []
    inner = range(1, last)
    for j, i in sorted(((j, i) for j in inner for i in inner if j != i), key=lambda p: (abs(p[0] - p[1]), p)):
        for chosen in sets:
            if all(j != a and i != b for a, b in chosen):
                chosen.append((j, i))
                break
        else:
            sets.append([(j, i)])
    out = [[(first, 1), (last, last - 1)]]
    for chosen in sets:
        out.append(chosen)
        out.append([({1: first, last - 1: last}[j], i) for j, i in chosen if j in (1, last - 1)])
    return out


def target_in(pairs, index):
    found = jnp.int32(0)
    for source, target in pairs:
        found = jnp.where(index == source, target, found)
    return found


def call(body, name, scalars, ins, in_specs, outs, out_specs, grid, scratch=(), after=(), aliases=None):
    count, skip = len(ins), len(after)

    def kernel(scalar_ref, *refs):
        body(scalar_ref, refs[:count], refs[count + skip :])

    return pl.pallas_call(
        kernel,
        name=name,
        out_shape=[jax.ShapeDtypeStruct(shape, dtype) for shape, dtype in outs],
        grid_spec=pltpu.PrefetchScalarGridSpec(
            num_scalar_prefetch=1,
            grid=grid,
            in_specs=list(in_specs) + [pl.BlockSpec(memory_space=pl.ANY)] * skip,
            out_specs=list(out_specs),
            scratch_shapes=list(scratch),
        ),
        input_output_aliases=aliases or {},
        compiler_params=pltpu.CompilerParams(
            dimension_semantics=("arbitrary",) * len(grid), vmem_limit_bytes=VMEM_LIMIT
        ),
        cost_estimate=pl.CostEstimate(flops=1, bytes_accessed=1, transcendentals=0),
    )(jnp.stack(scalars).astype(jnp.int32), *ins, *after)


def whole(shape):
    return pl.BlockSpec(shape, lambda j, s: (0,) * len(shape))


def earlier_mask(token_count):
    first = lax.broadcasted_iota(jnp.int32, (token_count, token_count), 0)
    second = lax.broadcasted_iota(jnp.int32, (token_count, token_count), 1)
    return jnp.where(first < second, 1.0, 0.0).astype(BF16)


def pair_in(ref, token_count):
    return ref[token_count:, :token_count].astype(F32).astype(jnp.int32)


def slot_marks(pair, expert, capacity, earlier):
    token_count = pair.shape[1]
    named = (pair[0:1] == expert) | (pair[1:2] == expert)
    named = jnp.broadcast_to(jnp.where(named, 1.0, 0.0), (capacity, token_count))
    rank = dot(named.astype(BF16), earlier)
    slot = lax.broadcasted_iota(jnp.int32, (capacity, token_count), 0).astype(F32)
    return jnp.where(rank == slot, named, 0.0).astype(BF16)


ROUTE_ROWS = 16


def cut_columns(rows, pair, group, targets, groups, block):
    def end_of(index):
        return jnp.where(index < groups // 2, 0, groups - 1)

    token_count, width = rows.shape
    lines = token_count + ROUTE_ROWS
    if block % 128:
        wide = -(-block // 128) * 128

        def tail(columns):
            return jnp.pad(pair.astype(BF16), ((0, ROUTE_ROWS - 2), (0, columns - token_count)))

        def cut(index):
            return jnp.concatenate([cut_padded(rows, [index], block, wide), tail(wide)], axis=0)

        return [jnp.concatenate([rows, tail(width)], axis=0)] + [
            jnp.concatenate([cut(t)] + ([cut(end_of(t))] if k else []), axis=1) for k, t in enumerate(targets)
        ]
    scalars = targets + [end_of(t) for t in targets[1:]]
    count = len(targets)

    def body(s, ins, outs):
        held = jnp.concatenate([ins[0][...].astype(F32), jnp.zeros((ROUTE_ROWS - 2, token_count), F32)], axis=0)
        for i, o in zip(ins[1:], outs):
            o[:token_count] = i[...]
            o[token_count:] = jnp.zeros((ROUTE_ROWS, block), BF16)
            o[token_count:, :token_count] = held.astype(BF16)

    def from_block(k):
        if k == 0:
            return lambda j, s: (0, s[0])
        return lambda j, s: (0, jnp.where(j == 0, s[k], s[count + k - 1]))

    return call(
        body,
        "cut_columns",
        scalars,
        [pair] + [rows] * (count + 1),
        [whole(pair.shape), pl.BlockSpec((token_count, block), lambda j, s: (0, j))]
        + [pl.BlockSpec((token_count, block), from_block(k)) for k in range(count)],
        [((lines, width), BF16)] + [((lines, block * (1 if k == 0 else 2)), BF16) for k in range(count)],
        [pl.BlockSpec((lines, block), lambda j, s: (0, j))]
        + [
            pl.BlockSpec(
                (lines, block), (lambda j, s: (0, 0)) if k == 0 else (lambda j, s: (0, jnp.minimum(j, 1)))
            )
            for k in range(count)
        ],
        (groups,),
    )


def cut_padded(rows, indices, block, wide):
    pieces = [lax.dynamic_slice_in_dim(rows, i * block, block, axis=1) for i in indices]
    return jnp.concatenate([jnp.pad(p, ((0, 0), (0, wide - block))) for p in pieces], axis=1)


def forward(expert, places, rows, upstream, gate_w, up_w, up_parts, first=None, after=()):
    sources = len(rows)
    lines, width = rows[0].shape
    token_count = lines - ROUTE_ROWS
    slots, hidden = upstream.shape
    capacity = slots // len(places)
    skip = 0 if first is None else len(places) - sources
    used = places[skip : skip + sources]
    step = 256 if hidden % 256 == 0 else hidden
    count = sources * capacity
    lead = skip * capacity
    spans, at = [], 0
    for size in up_parts:
        spans.append((at // step, (at + size) // step))
        at += size

    def body(s, ins, refs):
        tok = ins[:sources]
        up_ref, wg, wu = ins[sources : sources + 3]
        gate_out, up_outs, received = refs[0], refs[1:-1], refs[-1]
        j = pl.program_id(0)

        @pl.when(pl.program_id(0) == 0)
        def _():
            earlier = earlier_mask(token_count)
            for r in range(sources):
                mark = slot_marks(pair_in(tok[r], token_count), s[0], capacity, earlier)
                received[r * capacity : (r + 1) * capacity] = dot(mark, tok[r][:token_count]).astype(BF16)

        gate = dot(received[...], wg[...])
        up = dot(received[...], wu[...])
        for r in range(sources):
            here = slice(r * capacity, (r + 1) * capacity)
            g = gate[here]
            h = up_ref[pl.ds(pl.multiple_of(s[1 + r] * capacity, 16), capacity), :].astype(F32)
            sig = jax.nn.sigmoid(g)
            gate_out[here] = (h * up[here] * sig * (1.0 + g * (1.0 - sig))).astype(BF16)
            up_grad = (h * g * sig).astype(BF16)
            for (low, high), out in zip(spans, up_outs):

                @pl.when((j >= low) & (j < high))
                def _():
                    out[lead + r * capacity : lead + (r + 1) * capacity] = up_grad

        if first is not None:
            for (low, high), out in zip(spans, up_outs):

                @pl.when((j >= low) & (j < high))
                def _():
                    out[:lead] = ins[sources + 3][...]

    ins = list(rows) + [upstream, gate_w, up_w]
    specs = [whole((lines, width))] * sources
    specs += [pl.BlockSpec((slots, step), lambda j, s: (0, j))]
    specs += [pl.BlockSpec((width, step), lambda j, s: (0, j))] * 2
    if first is not None:
        ins.append(first)
        specs.append(pl.BlockSpec((lead, step), lambda j, s: (0, j)))
    return call(
        body,
        "forward_first" if first is None else "forward_rest",
        [expert] + used,
        ins,
        specs,
        [((count, hidden), BF16)] + [((lead + count, size), BF16) for size in up_parts],
        [pl.BlockSpec((count, step), lambda j, s: (0, j))]
        + [
            pl.BlockSpec((lead + count, step), lambda j, s, a=low, b=high: (0, jnp.clip(j - a, 0, b - a - 1)))
            for low, high in spans
        ],
        (hidden // step,),
        scratch=[pltpu.VMEM((count, width), BF16)],
        after=after,
    )


def halves_of(width):
    step = 512 if width % 512 == 0 else 128
    steps = width // step
    return step, steps, (steps + 1) // 2


def slot_gradients(places, gate_parts, up_parts, gate_w, up_w, after=()):
    width, hidden = gate_w.shape
    slots = up_parts[0].shape[0]
    capacity = slots // len(places)
    gates = len(gate_parts)
    step, steps, lead = halves_of(width)

    def body(s, ins, outs):
        j = pl.program_id(0)
        wg, wu = ins[-2], ins[-1]
        across = ((1,), (1,))
        total = jnp.concatenate([dot(g[...], wg[...], across) for g in ins[:gates]], axis=0)
        at = 0
        for g in ins[gates:-2]:
            size = g.shape[1]
            total = total + dot(g[...], wu[:, at : at + size], across)
            at += size
        total = total.astype(BF16)

        def put(out):
            for r in range(len(places)):
                at = pl.ds(pl.multiple_of(s[r] * capacity, 16), capacity)
                out[at, :] = total[r * capacity : (r + 1) * capacity]

        @pl.when(j < lead)
        def _():
            put(outs[0])

        @pl.when(j >= lead)
        def _():
            put(outs[1])

    return call(
        body,
        "slot_gradients",
        places,
        list(gate_parts) + list(up_parts) + [gate_w, up_w],
        [whole(g.shape) for g in list(gate_parts) + list(up_parts)]
        + [pl.BlockSpec((step, hidden), lambda j, s: (j, 0))] * 2,
        [((slots, lead * step), BF16), ((slots, width - lead * step), BF16)],
        [
            pl.BlockSpec((slots, step), lambda j, s: (0, jnp.minimum(j, lead - 1))),
            pl.BlockSpec((slots, step), lambda j, s: (0, jnp.maximum(j - lead, 0))),
        ],
        (steps,),
        after=after,
    )


def combine(pair, returned, experts, after=()):
    token_count = pair.shape[1]
    slots, width = returned.shape
    capacity = slots // experts
    step = 512 if width % 512 == 0 else 128

    def body(s, ins, refs):
        marks = refs[-1]

        @pl.when(pl.program_id(0) == 0)
        def _():
            earlier = earlier_mask(token_count)
            for r in range(experts):
                marks[r * capacity : (r + 1) * capacity] = slot_marks(ins[0][...], r, capacity, earlier)

        refs[0][...] = dot(marks[...], ins[1][...], ((0,), (0,))).astype(BF16)

    return call(
        body,
        "combine",
        [jnp.int32(0)],
        [pair, returned],
        [whole(pair.shape), pl.BlockSpec((slots, step), lambda j, s: (0, j))],
        [((token_count, width), BF16)],
        [pl.BlockSpec((token_count, step), lambda j, s: (0, j))],
        (width // step,),
        scratch=[pltpu.VMEM((slots, token_count), BF16)],
        after=after,
    )[0]


def pick_rows(expert, blocks, rows, capacity, block, routes=None, after=()):
    sources = len(rows)
    lines = rows[0].shape[0]
    token_count = lines - ROUTE_ROWS
    count = len(blocks)

    def body(s, ins, outs):
        earlier = earlier_mask(token_count)
        picked = []
        for r in range(sources):
            pair = pair_in(ins[r], token_count) if routes is None else ins[sources + r][...]
            pair = pair.astype(F32).astype(jnp.int32)
            mark = slot_marks(pair, s[0], capacity, earlier)
            picked.append(dot(mark, ins[r][:token_count]))
        outs[0][...] = jnp.concatenate(picked, axis=0).astype(BF16).T

    ins, specs = list(rows), []
    for r in range(sources):
        specs.append(pl.BlockSpec((lines, block), lambda j, s: (0, s[1 + j])))
    if routes is not None:
        ins += list(routes)
        specs += [
            pl.BlockSpec((ROUTE_ROWS, token_count), lambda j, s: (token_count // ROUTE_ROWS, 0)) for _ in routes
        ]
    return call(
        body,
        "pick_rows",
        [expert] + list(blocks),
        ins,
        specs,
        [((count * block, sources * capacity), BF16)],
        [pl.BlockSpec((block, sources * capacity), lambda j, s: (j, 0))],
        (count,),
        after=after,
    )[0]


def products(terms, block, part, dtype, name, extras=(), total=None, after=()):
    slots = terms[0][0].shape[1]
    split = 2 if block % 32 == 0 else 1
    lines = block // split

    def body(s, ins, outs):
        at, result = len(terms), None
        for k, (_, _, parts) in enumerate(terms):
            row = 0
            for _ in parts:
                g = ins[at]
                new = dot(ins[k][:, row : row + g.shape[0]] if len(parts) > 1 else ins[k][...], g[...])
                result = new if result is None else result + new
                row += g.shape[0]
                at += 1
        if extras:
            result = result + jnp.concatenate([e[...].astype(F32) for e in ins[at:]], axis=1)
        outs[0][...] = result.astype(dtype)

    ins = [p for p, _, _ in terms]
    specs = [pl.BlockSpec((lines, slots), lambda j, s, i=i: (i * split + j, 0)) for _, i, _ in terms]
    for _, _, parts in terms:
        for array, column in parts:
            ins.append(array)
            specs.append(pl.BlockSpec((array.shape[0], part), lambda j, s, c=column: (0, c)))
    for e in extras:
        ins.append(e)
        specs.append(pl.BlockSpec((lines, e.shape[1]), lambda j, s: (j, 0)))
    return call(
        body,
        name,
        [jnp.int32(0)],
        ins,
        specs,
        [((block, total or part), dtype)],
        [pl.BlockSpec((lines, part), lambda j, s: (j, 0))],
        (split,),
        after=after,
    )[0]


def finish(own, extra, target, place, total, after=()):
    block, part = own.shape
    ins = [own, extra]
    specs = [whole((block, part))] * 2
    if target is not None:
        ins.append(target)
        specs.append(pl.BlockSpec(memory_space=pl.ANY))

    def body(s, refs, outs):
        outs[0][...] = (refs[0][...] + refs[1][...].astype(F32)).astype(BF16)

    return call(
        body,
        "finish",
        [jnp.int32(0)],
        ins,
        specs,
        [((block, total), BF16)],
        [pl.BlockSpec((block, part), lambda j, s: (0, place))],
        (1,),
        after=after,
        aliases={3: 0} if target is not None else None,
    )[0]


def tied(value, *others):
    return lax.optimization_barrier((value,) + others)[0]


def shards(tokens, routes, hidden_grad, w_gate, w_up):
    groups = lax.axis_size("dp")
    experts = lax.axis_size("expert")
    sections = lax.axis_size("section")
    group = lax.axis_index("dp")
    expert = lax.axis_index("expert")
    rows = tokens[0]
    token_count, width = rows.shape
    slots = hidden_grad.shape[3]
    capacity = slots // experts
    hidden = w_gate.shape[3]
    block = width // groups
    gate_w = w_gate[0, 0]
    up_w = w_up[0, 0]
    upstream = hidden_grad[0, 0, 0]
    sets = grouped_pairs(groups)
    up_parts = [hidden // 2, hidden // 2]
    wide = -(-block // 128) * 128
    own_blocks = [group, jnp.where(group < groups // 2, 0, groups - 1)]

    def swap(value):
        return lax.ppermute(value, "expert", [(s, s ^ 1) for s in range(experts)])

    def shift(value, by):
        return lax.ppermute(value, "expert", [(s, (s + 2 * by) % experts) for s in range(experts)])

    def over_groups(value, pairs):
        return lax.ppermute(value, "dp", pairs)

    def to_sources(value):
        back = lax.all_to_all(
            value.reshape(experts, capacity, value.shape[1]), "expert", split_axis=0, concat_axis=0, tiled=True
        )
        return back.reshape(value.shape)

    def passed_on(value):
        return lax.ppermute(value, "section", [(s, (s - 1) % sections) for s in range(sections)])

    def to_ends(value):
        return lax.ppermute(value, "dp", [(1, 0), (groups - 2, groups - 1)])

    chips = range(1, experts // 2)
    places = [jnp.bitwise_xor((expert - 2 * (r // 2)) % experts, r % 2) for r in range(experts)]
    targets = [target_in(pairs, group) for pairs in sets]
    order = list(range(1, len(sets))) + [0]

    pair = routes[0].T
    own, *cut = cut_columns(rows, pair, group, targets, groups, block)
    far_even = [shift(own, by) for by in chips]
    others = {k: over_groups(cut[k], sets[k]) for k in order}
    partner = swap(own)
    near_gate, near_up = forward(expert, places, [own, partner], upstream, gate_w, up_w, [hidden])
    epoch = [others[k] for k in order] + far_even + [near_gate]

    near_sent = {k: over_groups(tied(near_gate, *epoch), sets[k]) for k in order}
    far = []
    for value in far_even:
        far += [value, swap(tied(value, *epoch))]
    end_columns = jnp.concatenate([others[k][:, wide:] for k in range(1, len(sets))], axis=1)
    own_part = jnp.concatenate([others[k][:, :wide] for k in range(len(sets))], axis=1)
    end_columns = tied(end_columns, *epoch)
    end_far = [shift(end_columns, by) for by in chips]
    far_gate, *ups = forward(
        expert,
        places,
        far,
        upstream,
        gate_w,
        up_w,
        up_parts,
        first=near_up,
        after=[near_gate, end_columns],
    )
    end_rows = [end_columns, swap(tied(end_columns, *far))]
    epoch = [near_sent[k] for k in order] + end_far + [far_gate, end_rows[1]]

    far_sent = {k: over_groups(tied(far_gate, *epoch), sets[k]) for k in order}
    for value in end_far:
        end_rows += [value, swap(tied(value, *epoch))]
    own_part = tied(own_part, *epoch)
    column_rows = [own_part]
    column_far = [shift(own_part, by) for by in chips]
    first_back, second_back = slot_gradients(
        places, [near_gate, far_gate], ups, gate_w, up_w, after=[end_rows[-1]]
    )
    first_back = to_sources(first_back)
    own_columns = [own, partner] + far
    own_lines = own_columns
    if wide != block:
        own_columns = [cut_padded(v, own_blocks, block, wide) for v in own_columns]
        own_blocks = [jnp.int32(0), jnp.int32(1)]
    own_picked = pick_rows(
        expert, own_blocks, own_columns, capacity, wide, routes=own_lines, after=[second_back]
    )
    column_rows.append(swap(tied(own_part, *end_rows)))
    end_picked = pick_rows(
        expert, [jnp.int32(k) for k in range(len(sets) - 1)], end_rows, capacity, wide, after=[own_picked]
    )
    epoch = [far_sent[k] for k in order] + [end_picked] + column_far + column_rows

    def parts_of(c):
        if c < 2:
            out = [[(near_gate, c), (far_gate, c)]]
            out += [[(near_sent[k], c), (far_sent[k], c)] for k in range(len(sets))]
        else:
            out = [[(ups[c - 2], 0)]] + [[(up_sent[c - 2][k], 0)] for k in range(len(sets))]
        return out

    def for_end(c, after):
        parts = parts_of(c)
        part = hidden // 2 if c < 2 else up_parts[c - 2]
        terms = [(own_picked, 1, parts[0])]
        terms += [(end_picked, k - 1, parts[1 + k]) for k in range(1, len(sets))]
        return products(terms, wide, part, BF16, "for_end", after=after)

    def for_own(c, part, dtype, after, extras=(), total=None):
        parts = parts_of(c)
        terms = [(own_picked, 0, parts[0])]
        terms += [(picked, k, parts[1 + k]) for k in range(len(sets))]
        return products(terms, wide, part, dtype, "for_own", extras=extras, total=total, after=after)

    up_sent = []

    def send_up(c):
        up_sent.append({k: over_groups(tied(ups[c], *epoch), sets[k]) for k in order})
        return [up_sent[c][k] for k in order]

    arriving = send_up(0)
    for value in column_far:
        column_rows += [value, swap(tied(value, *epoch))]
    end0 = for_end(0, epoch[:1])
    extra0 = to_ends(end0)
    end1 = for_end(1, [end0])
    extra1 = to_ends(tied(end1, *column_rows))
    picked = pick_rows(
        expert, [jnp.int32(k) for k in range(len(sets))], column_rows, capacity, wide, after=[end1]
    )
    epoch = arriving + [picked, extra0]

    arriving = send_up(1)
    second_back = to_sources(tied(second_back, first_back, *epoch))
    end2 = for_end(2, epoch[:1])
    extra2 = to_ends(end2)
    first_tok = combine(pair, first_back, experts, after=[end2])
    first_passed = passed_on(tied(first_tok, extra1))
    gate = for_own(0, hidden, BF16, [first_tok], extras=[extra0, extra1])
    epoch = arriving + [gate]

    end3 = for_end(3, epoch)
    extra3 = to_ends(end3)
    second_tok = combine(pair, second_back, experts, after=[end3])
    second_passed = passed_on(second_tok)
    up0 = for_own(2, up_parts[0], BF16, [second_tok], extras=[extra2], total=hidden)
    own3 = for_own(3, up_parts[1], F32, [up0])
    passed = jnp.concatenate([tied(first_passed, own3), second_passed], axis=1)
    up1 = finish(own3, extra3, up0, up_parts[0] // up_parts[1], hidden)
    return (passed[None], gate[None, None, :block], up1[None, None, :block])


def solution(mesh):
    placed = (
        P("section", ("dp", "expert"), None),
        P("section", ("dp", "expert"), None),
        P("section", "dp", "expert", None, None),
        P("section", "expert", None, None),
        P("section", "expert", None, None),
    )
    return jax.shard_map(
        shards,
        mesh=mesh,
        in_specs=placed,
        out_specs=(
            P("section", ("dp", "expert"), None),
            P("section", "expert", "dp", None),
            P("section", "expert", "dp", None),
        ),
        check_vma=False,
    )
```

```python
import jax
import jax.numpy as jnp
from jax import lax
from jax.experimental import pallas as pl
from jax.experimental.pallas import tpu as pltpu
from jax.sharding import PartitionSpec as P

BF16 = jnp.bfloat16
F32 = jnp.float32
MIB = 1024 * 1024


def dot(a, b, contract=((1,), (0,))):
    return lax.dot_general(a, b, (contract, ((), ())), preferred_element_type=F32)


def grouped_pairs(count):
    first, last = 0, count - 1
    sets = []
    inner = range(1, last)
    for j, i in sorted(((j, i) for j in inner for i in inner if j != i), key=lambda p: (abs(p[0] - p[1]), p)):
        for chosen in sets:
            if all(j != a and i != b for a, b in chosen):
                chosen.append((j, i))
                break
        else:
            sets.append([(j, i)])
    out = [[(first, 1), (last, last - 1)]]
    for chosen in sets:
        out.append(chosen)
        out.append([({1: first, last - 1: last}[j], i) for j, i in chosen if j in (1, last - 1)])
    return out


def target_in(pairs, index):
    found = jnp.int32(0)
    for source, target in pairs:
        found = jnp.where(index == source, target, found)
    return found


def call(body, name, scalars, ins, in_specs, outs, out_specs, grid, scratch=(), after=(), aliases=None, vmem=28):
    count, skip = len(ins), len(after)

    def kernel(scalar_ref, *refs):
        body(scalar_ref, refs[:count], refs[count + skip :])

    return pl.pallas_call(
        kernel,
        name=name,
        out_shape=[jax.ShapeDtypeStruct(shape, dtype) for shape, dtype in outs],
        grid_spec=pltpu.PrefetchScalarGridSpec(
            num_scalar_prefetch=1,
            grid=grid,
            in_specs=list(in_specs) + [pl.BlockSpec(memory_space=pl.ANY)] * skip,
            out_specs=list(out_specs),
            scratch_shapes=list(scratch),
        ),
        input_output_aliases=aliases or {},
        compiler_params=pltpu.CompilerParams(
            dimension_semantics=("arbitrary",) * len(grid), vmem_limit_bytes=vmem * MIB
        ),
        cost_estimate=pl.CostEstimate(flops=1, bytes_accessed=1, transcendentals=0),
    )(jnp.stack(scalars).astype(jnp.int32), *ins, *after)


def whole(shape):
    return pl.BlockSpec(shape, lambda j, s: (0,) * len(shape))


def earlier_mask(token_count):
    first = lax.broadcasted_iota(jnp.int32, (token_count, token_count), 0)
    second = lax.broadcasted_iota(jnp.int32, (token_count, token_count), 1)
    return jnp.where(first < second, 1.0, 0.0).astype(BF16)


def pair_in(ref, token_count):
    return ref[token_count:, :token_count].astype(F32).astype(jnp.int32)


def slot_marks(pair, expert, capacity, earlier):
    token_count = pair.shape[1]
    named = (pair[0:1] == expert) | (pair[1:2] == expert)
    named = jnp.broadcast_to(jnp.where(named, 1.0, 0.0), (capacity, token_count))
    rank = dot(named.astype(BF16), earlier)
    slot = lax.broadcasted_iota(jnp.int32, (capacity, token_count), 0).astype(F32)
    return jnp.where(rank == slot, named, 0.0).astype(BF16)


ROUTE_ROWS = 16


def cut_columns(rows, pair, group, targets, groups, block):
    def end_of(index):
        return jnp.where(index < groups // 2, 0, groups - 1)

    token_count, width = rows.shape
    lines = token_count + ROUTE_ROWS
    if block % 128:
        wide = -(-block // 128) * 128

        def tail(columns):
            return jnp.pad(pair.astype(BF16), ((0, ROUTE_ROWS - 2), (0, columns - token_count)))

        def cut(index):
            return jnp.concatenate([cut_padded(rows, [index], block, wide), tail(wide)], axis=0)

        return [jnp.concatenate([rows, tail(width)], axis=0)] + [
            jnp.concatenate([cut(t)] + ([cut(end_of(t))] if k else []), axis=1) for k, t in enumerate(targets)
        ]
    scalars = targets + [end_of(t) for t in targets[1:]]
    count = len(targets)

    def body(s, ins, outs):
        held = jnp.concatenate([ins[0][...].astype(F32), jnp.zeros((ROUTE_ROWS - 2, token_count), F32)], axis=0)
        for i, o in zip(ins[1:], outs):
            o[:token_count] = i[...]
            o[token_count:] = jnp.zeros((ROUTE_ROWS, block), BF16)
            o[token_count:, :token_count] = held.astype(BF16)

    def from_block(k):
        if k == 0:
            return lambda j, s: (0, s[0])
        return lambda j, s: (0, jnp.where(j == 0, s[k], s[count + k - 1]))

    return call(
        body,
        "cut_columns",
        scalars,
        [pair] + [rows] * (count + 1),
        [whole(pair.shape), pl.BlockSpec((token_count, block), lambda j, s: (0, j))]
        + [pl.BlockSpec((token_count, block), from_block(k)) for k in range(count)],
        [((lines, width), BF16)] + [((lines, block * (1 if k == 0 else 2)), BF16) for k in range(count)],
        [pl.BlockSpec((lines, block), lambda j, s: (0, j))]
        + [
            pl.BlockSpec(
                (lines, block), (lambda j, s: (0, 0)) if k == 0 else (lambda j, s: (0, jnp.minimum(j, 1)))
            )
            for k in range(count)
        ],
        (groups,),
    )


def cut_padded(rows, indices, block, wide):
    pieces = [lax.dynamic_slice_in_dim(rows, i * block, block, axis=1) for i in indices]
    return jnp.concatenate([jnp.pad(p, ((0, 0), (0, wide - block))) for p in pieces], axis=1)


def forward(expert, places, rows, upstream, gate_w, up_w, up_parts, first=None, after=()):
    sources = len(rows)
    lines, width = rows[0].shape
    token_count = lines - ROUTE_ROWS
    slots, hidden = upstream.shape
    capacity = slots // len(places)
    skip = 0 if first is None else len(places) - sources
    used = places[skip : skip + sources]
    step = 256 if hidden % 256 == 0 else hidden
    count = sources * capacity
    lead = skip * capacity
    spans, at = [], 0
    for size in up_parts:
        spans.append((at // step, (at + size) // step))
        at += size

    def body(s, ins, refs):
        tok = ins[:sources]
        up_ref, wg, wu = ins[sources : sources + 3]
        gate_out, up_outs, received = refs[0], refs[1:-1], refs[-1]
        j = pl.program_id(0)

        @pl.when(pl.program_id(0) == 0)
        def _():
            earlier = earlier_mask(token_count)
            for r in range(sources):
                mark = slot_marks(pair_in(tok[r], token_count), s[0], capacity, earlier)
                received[r * capacity : (r + 1) * capacity] = dot(mark, tok[r][:token_count]).astype(BF16)

        gate = dot(received[...], wg[...])
        up = dot(received[...], wu[...])
        for r in range(sources):
            here = slice(r * capacity, (r + 1) * capacity)
            g = gate[here]
            h = up_ref[pl.ds(pl.multiple_of(s[1 + r] * capacity, 16), capacity), :].astype(F32)
            sig = jax.nn.sigmoid(g)
            gate_out[here] = (h * up[here] * sig * (1.0 + g * (1.0 - sig))).astype(BF16)
            up_grad = (h * g * sig).astype(BF16)
            for (low, high), out in zip(spans, up_outs):

                @pl.when((j >= low) & (j < high))
                def _():
                    out[lead + r * capacity : lead + (r + 1) * capacity] = up_grad

        if first is not None:
            for (low, high), out in zip(spans, up_outs):

                @pl.when((j >= low) & (j < high))
                def _():
                    out[:lead] = ins[sources + 3][...]

    ins = list(rows) + [upstream, gate_w, up_w]
    specs = [whole((lines, width))] * sources
    specs += [pl.BlockSpec((slots, step), lambda j, s: (0, j))]
    specs += [pl.BlockSpec((width, step), lambda j, s: (0, j))] * 2
    if first is not None:
        ins.append(first)
        specs.append(pl.BlockSpec((lead, step), lambda j, s: (0, j)))
    return call(
        body,
        "forward_first" if first is None else "forward_rest",
        [expert] + used,
        ins,
        specs,
        [((count, hidden), BF16)] + [((lead + count, size), BF16) for size in up_parts],
        [pl.BlockSpec((count, step), lambda j, s: (0, j))]
        + [
            pl.BlockSpec((lead + count, step), lambda j, s, a=low, b=high: (0, jnp.clip(j - a, 0, b - a - 1)))
            for low, high in spans
        ],
        (hidden // step,),
        scratch=[pltpu.VMEM((count, width), BF16)],
        after=after,
        vmem=56,
    )


def halves_of(width):
    step = 512 if width % 512 == 0 else 128
    steps = width // step
    return step, steps, (steps + 1) // 2


def slot_gradients(places, gate, ups, gate_w, up_w, near=None, after=()):
    width, hidden = gate_w.shape
    count = gate.shape[0]
    skip = 0 if near is None else near.shape[0]
    slots = skip + count
    capacity = slots // len(places) if skip else count // 2
    step, steps, lead = halves_of(width)

    def body(s, ins, outs):
        j = pl.program_id(0)
        wg, wu = ins[0], ins[1]
        across = ((1,), (1,))
        total = dot(ins[2][...], wg[...], across)
        at = 0
        for g in ins[3 : 3 + len(ups)]:
            size = g.shape[1]
            total = total + dot(g[skip:], wu[:, at : at + size], across)
            at += size
        total = total.astype(BF16)
        if near is None:
            outs[0][...] = total
            return

        def put(out):
            for r in range(len(places)):
                at = pl.ds(pl.multiple_of(s[r] * capacity, 16), capacity)
                if r < 2:
                    out[at, :] = ins[-1][r * capacity : (r + 1) * capacity]
                else:
                    out[at, :] = total[(r - 2) * capacity : (r - 1) * capacity]

        @pl.when(j < lead)
        def _():
            put(outs[0])

        @pl.when(j >= lead)
        def _():
            put(outs[1])

    ins = [gate_w, up_w, gate] + list(ups)
    specs = [pl.BlockSpec((step, hidden), lambda j, s: (j, 0))] * 2 + [whole(g.shape) for g in ins[2:]]
    if near is None:
        outs = [((slots, width), BF16)]
        out_specs = [pl.BlockSpec((slots, step), lambda j, s: (0, j))]
    else:
        ins.append(near)
        specs.append(pl.BlockSpec((skip, step), lambda j, s: (0, j)))
        outs = [((slots, lead * step), BF16), ((slots, width - lead * step), BF16)]
        out_specs = [
            pl.BlockSpec((slots, step), lambda j, s: (0, jnp.minimum(j, lead - 1))),
            pl.BlockSpec((slots, step), lambda j, s: (0, jnp.maximum(j - lead, 0))),
        ]
    out = call(
        body,
        "near_gradients" if near is None else "slot_gradients",
        places,
        ins,
        specs,
        outs,
        out_specs,
        (steps,),
        after=after,
        vmem=56,
    )
    return out[0] if near is None else out


def combine(pair, returned, experts, after=()):
    token_count = pair.shape[1]
    slots, width = returned.shape
    capacity = slots // experts
    step = 512 if width % 512 == 0 else 128

    def body(s, ins, refs):
        marks = refs[-1]

        @pl.when(pl.program_id(0) == 0)
        def _():
            earlier = earlier_mask(token_count)
            for r in range(experts):
                marks[r * capacity : (r + 1) * capacity] = slot_marks(ins[0][...], r, capacity, earlier)

        refs[0][...] = dot(marks[...], ins[1][...], ((0,), (0,))).astype(BF16)

    return call(
        body,
        "combine",
        [jnp.int32(0)],
        [pair, returned],
        [whole(pair.shape), pl.BlockSpec((slots, step), lambda j, s: (0, j))],
        [((token_count, width), BF16)],
        [pl.BlockSpec((token_count, step), lambda j, s: (0, j))],
        (width // step,),
        scratch=[pltpu.VMEM((slots, token_count), BF16)],
        after=after,
    )[0]


def pick_rows(expert, blocks, rows, capacity, block, routes=None, after=()):
    sources = len(rows)
    lines = rows[0].shape[0]
    token_count = lines - ROUTE_ROWS
    count = len(blocks)

    def body(s, ins, outs):
        earlier = earlier_mask(token_count)
        picked = []
        for r in range(sources):
            pair = pair_in(ins[r], token_count) if routes is None else ins[sources + r][...]
            pair = pair.astype(F32).astype(jnp.int32)
            mark = slot_marks(pair, s[0], capacity, earlier)
            picked.append(dot(mark, ins[r][:token_count]))
        outs[0][...] = jnp.concatenate(picked, axis=0).astype(BF16).T

    ins, specs = list(rows), []
    for r in range(sources):
        specs.append(pl.BlockSpec((lines, block), lambda j, s: (0, s[1 + j])))
    if routes is not None:
        ins += list(routes)
        specs += [
            pl.BlockSpec((ROUTE_ROWS, token_count), lambda j, s: (token_count // ROUTE_ROWS, 0)) for _ in routes
        ]
    return call(
        body,
        "pick_rows",
        [expert] + list(blocks),
        ins,
        specs,
        [((count * block, sources * capacity), BF16)],
        [pl.BlockSpec((block, sources * capacity), lambda j, s: (j, 0))],
        (count,),
        after=after,
    )[0]


def products(terms, block, part, dtype, name, extras=(), total=None, after=()):
    slots = terms[0][0].shape[1]
    split = 2 if block % 32 == 0 else 1
    lines = block // split

    def body(s, ins, outs):
        at, result = len(terms), None
        for k, (_, _, parts) in enumerate(terms):
            row = 0
            for _ in parts:
                g = ins[at]
                new = dot(ins[k][:, row : row + g.shape[0]] if len(parts) > 1 else ins[k][...], g[...])
                result = new if result is None else result + new
                row += g.shape[0]
                at += 1
        if extras:
            result = result + jnp.concatenate([e[...].astype(F32) for e in ins[at:]], axis=1)
        outs[0][...] = result.astype(dtype)

    ins = [p for p, _, _ in terms]
    specs = [pl.BlockSpec((lines, slots), lambda j, s, i=i: (i * split + j, 0)) for _, i, _ in terms]
    for _, _, parts in terms:
        for array, column in parts:
            ins.append(array)
            specs.append(pl.BlockSpec((array.shape[0], part), lambda j, s, c=column: (0, c)))
    for e in extras:
        ins.append(e)
        specs.append(pl.BlockSpec((lines, e.shape[1]), lambda j, s: (j, 0)))
    return call(
        body,
        name,
        [jnp.int32(0)],
        ins,
        specs,
        [((block, total or part), dtype)],
        [pl.BlockSpec((lines, part), lambda j, s: (j, 0))],
        (split,),
        after=after,
    )[0]


def finish(own, extra, target, place, total, after=()):
    block, part = own.shape
    ins = [own, extra]
    specs = [whole((block, part))] * 2
    if target is not None:
        ins.append(target)
        specs.append(pl.BlockSpec(memory_space=pl.ANY))

    def body(s, refs, outs):
        outs[0][...] = (refs[0][...] + refs[1][...].astype(F32)).astype(BF16)

    return call(
        body,
        "finish",
        [jnp.int32(0)],
        ins,
        specs,
        [((block, total), BF16)],
        [pl.BlockSpec((block, part), lambda j, s: (0, place))],
        (1,),
        after=after,
        aliases={3: 0} if target is not None else None,
    )[0]


def tied(value, *others):
    return lax.optimization_barrier((value,) + others)[0]


def shards(tokens, routes, hidden_grad, w_gate, w_up):
    groups = lax.axis_size("dp")
    experts = lax.axis_size("expert")
    sections = lax.axis_size("section")
    group = lax.axis_index("dp")
    expert = lax.axis_index("expert")
    rows = tokens[0]
    token_count, width = rows.shape
    slots = hidden_grad.shape[3]
    capacity = slots // experts
    hidden = w_gate.shape[3]
    block = width // groups
    gate_w = w_gate[0, 0]
    up_w = w_up[0, 0]
    upstream = hidden_grad[0, 0, 0]
    sets = grouped_pairs(groups)
    up_parts = [hidden // 2, hidden // 2]
    wide = -(-block // 128) * 128
    own_blocks = [group, jnp.where(group < groups // 2, 0, groups - 1)]

    def swap(value):
        return lax.ppermute(value, "expert", [(s, s ^ 1) for s in range(experts)])

    def shift(value, by):
        return lax.ppermute(value, "expert", [(s, (s + 2 * by) % experts) for s in range(experts)])

    def over_groups(value, pairs):
        return lax.ppermute(value, "dp", pairs)

    def to_sources(value):
        back = lax.all_to_all(
            value.reshape(experts, capacity, value.shape[1]), "expert", split_axis=0, concat_axis=0, tiled=True
        )
        return back.reshape(value.shape)

    def passed_on(value):
        return lax.ppermute(value, "section", [(s, (s - 1) % sections) for s in range(sections)])

    def to_ends(value):
        return lax.ppermute(value, "dp", [(1, 0), (groups - 2, groups - 1)])

    chips = range(1, experts // 2)
    places = [jnp.bitwise_xor((expert - 2 * (r // 2)) % experts, r % 2) for r in range(experts)]
    targets = [target_in(pairs, group) for pairs in sets]
    order = list(range(1, len(sets))) + [0]

    pair = routes[0].T
    own, *cut = cut_columns(rows, pair, group, targets, groups, block)
    far_even = [shift(own, by) for by in chips]
    others = {k: over_groups(cut[k], sets[k]) for k in order}
    partner = swap(own)
    near_gate, near_up = forward(expert, places, [own, partner], upstream, gate_w, up_w, [hidden])
    near_back = slot_gradients(places, near_gate, [near_up], gate_w, up_w, after=[near_gate])
    epoch = [others[k] for k in order] + far_even + [near_back]

    near_sent = {k: over_groups(tied(near_gate, *epoch), sets[k]) for k in order}
    far = []
    for value in far_even:
        far += [value, swap(tied(value, *epoch))]
    end_columns = tied(others[order[0]], far[-1])
    end_columns = jnp.concatenate(
        [end_columns[:, wide:]] + [others[k][:, wide:] for k in range(1, len(sets)) if k != order[0]], axis=1
    )
    end_far = [shift(end_columns, by) for by in chips]
    far_gate, *ups = forward(
        expert, places, far, upstream, gate_w, up_w, up_parts, first=near_up, after=[near_back]
    )
    own_columns = [own, partner] + far
    own_lines = own_columns
    if wide != block:
        own_columns = [cut_padded(v, own_blocks, block, wide) for v in own_columns]
        own_blocks = [jnp.int32(0), jnp.int32(1)]
    own_picked = pick_rows(
        expert, own_blocks, own_columns, capacity, wide, routes=own_lines, after=[far_gate]
    )
    epoch = [near_sent[k] for k in order] + [own_picked]

    far_sent = {k: over_groups(tied(far_gate, *epoch), sets[k]) for k in order}
    first_back, second_back = slot_gradients(
        places, far_gate, ups, gate_w, up_w, near=near_back, after=[own_picked]
    )
    first_back = to_sources(first_back)
    end_rows = []
    for value in [end_columns] + end_far:
        end_rows += [value, swap(tied(value, *epoch))]
    own_part = tied(others[0], *end_far)
    own_part = jnp.concatenate([own_part] + [others[k][:, :wide] for k in range(1, len(sets))], axis=1)
    column_far = [shift(own_part, by) for by in chips]
    end_picked = pick_rows(
        expert, [jnp.int32(k) for k in range(len(sets) - 1)], end_rows, capacity, wide, after=[second_back]
    )
    epoch = [far_sent[k] for k in order] + [end_picked]

    def parts_of(c):
        if c == 0:
            out = [[(near_gate, c), (far_gate, c)]]
            out += [[(near_sent[k], c), (far_sent[k], c)] for k in range(len(sets))]
        else:
            out = [[(ups[c - 1], 0)]] + [[(up_sent[c - 1][k], 0)] for k in range(len(sets))]
        return out

    def for_end(c, after):
        parts = parts_of(c)
        part = up_parts[c - 1] if c else hidden
        terms = [(own_picked, 1, parts[0])]
        terms += [(end_picked, k - 1, parts[1 + k]) for k in range(1, len(sets))]
        return products(terms, wide, part, BF16, "for_end", after=after)

    def for_own(c, part, dtype, after, extras=(), total=None):
        parts = parts_of(c)
        terms = [(own_picked, 0, parts[0])]
        terms += [(picked, k, parts[1 + k]) for k in range(len(sets))]
        return products(terms, wide, part, dtype, "for_own", extras=extras, total=total, after=after)

    up_sent = []

    def send_up(c):
        up_sent.append({k: over_groups(tied(ups[c], *epoch), sets[k]) for k in order})
        return [up_sent[c][k] for k in order]

    arriving = send_up(0)
    column_rows = []
    for value in [own_part] + column_far:
        column_rows += [value, swap(tied(value, *epoch))]
    end0 = for_end(0, [end_picked])
    extra0 = to_ends(end0)
    picked = pick_rows(
        expert, [jnp.int32(k) for k in range(len(sets))], column_rows, capacity, wide, after=[end0]
    )
    epoch = arriving + [picked, first_back]

    arriving = send_up(1)
    second_back = to_sources(tied(second_back, *epoch))
    end1 = for_end(1, [picked])
    extra1 = to_ends(end1)
    first_tok = combine(pair, first_back, experts, after=[end1])
    first_passed = passed_on(first_tok)
    gate = for_own(0, hidden, BF16, [first_tok], extras=[extra0])
    epoch = arriving + [gate]

    end2 = for_end(2, epoch)
    extra2 = to_ends(end2)
    second_tok = combine(pair, second_back, experts, after=[end2])
    second_passed = passed_on(second_tok)
    up0 = for_own(1, up_parts[0], BF16, [second_tok], extras=[extra1], total=hidden)
    own2 = for_own(2, up_parts[1], F32, [up0])
    passed = jnp.concatenate([tied(first_passed, own2), second_passed], axis=1)
    up1 = finish(own2, extra2, up0, up_parts[0] // up_parts[1], hidden)
    return (passed[None], gate[None, None, :block], up1[None, None, :block])


def solution(mesh):
    placed = (
        P("section", ("dp", "expert"), None),
        P("section", ("dp", "expert"), None),
        P("section", "dp", "expert", None, None),
        P("section", "expert", None, None),
        P("section", "expert", None, None),
    )
    return jax.shard_map(
        shards,
        mesh=mesh,
        in_specs=placed,
        out_specs=(
            P("section", ("dp", "expert"), None),
            P("section", "expert", "dp", None),
            P("section", "expert", "dp", None),
        ),
        check_vma=False,
    )
```

```python
import jax
import jax.numpy as jnp
from jax import lax
from jax.experimental import pallas as pl
from jax.experimental.pallas import tpu as pltpu
from jax.sharding import PartitionSpec as P

BF16 = jnp.bfloat16
F32 = jnp.float32
MIB = 1024 * 1024


def dot(a, b, contract=((1,), (0,))):
    return lax.dot_general(a, b, (contract, ((), ())), preferred_element_type=F32)


def grouped_pairs(count):
    first, last = 0, count - 1
    sets = []
    inner = range(1, last)
    for j, i in sorted(((j, i) for j in inner for i in inner if j != i), key=lambda p: (abs(p[0] - p[1]), p)):
        for chosen in sets:
            if all(j != a and i != b for a, b in chosen):
                chosen.append((j, i))
                break
        else:
            sets.append([(j, i)])
    out = [[(first, 1), (last, last - 1)]]
    for chosen in sets:
        out.append(chosen)
        out.append([({1: first, last - 1: last}[j], i) for j, i in chosen if j in (1, last - 1)])
    return out


def target_in(pairs, index):
    found = jnp.int32(0)
    for source, target in pairs:
        found = jnp.where(index == source, target, found)
    return found


def call(body, name, scalars, ins, in_specs, outs, out_specs, grid, scratch=(), after=(), aliases=None, vmem=28):
    count, skip = len(ins), len(after)

    def kernel(scalar_ref, *refs):
        body(scalar_ref, refs[:count], refs[count + skip :])

    return pl.pallas_call(
        kernel,
        name=name,
        out_shape=[jax.ShapeDtypeStruct(shape, dtype) for shape, dtype in outs],
        grid_spec=pltpu.PrefetchScalarGridSpec(
            num_scalar_prefetch=1,
            grid=grid,
            in_specs=list(in_specs) + [pl.BlockSpec(memory_space=pl.ANY)] * skip,
            out_specs=list(out_specs),
            scratch_shapes=list(scratch),
        ),
        input_output_aliases=aliases or {},
        compiler_params=pltpu.CompilerParams(
            dimension_semantics=("arbitrary",) * len(grid), vmem_limit_bytes=vmem * MIB
        ),
        cost_estimate=pl.CostEstimate(flops=1, bytes_accessed=1, transcendentals=0),
    )(jnp.stack(scalars).astype(jnp.int32), *ins, *after)


def whole(shape):
    return pl.BlockSpec(shape, lambda j, s: (0,) * len(shape))


def earlier_mask(token_count):
    first = lax.broadcasted_iota(jnp.int32, (token_count, token_count), 0)
    second = lax.broadcasted_iota(jnp.int32, (token_count, token_count), 1)
    return jnp.where(first < second, 1.0, 0.0).astype(BF16)


def pair_in(ref, token_count):
    return ref[token_count:, :token_count].astype(F32).astype(jnp.int32)


def slot_marks(pair, expert, capacity, earlier):
    token_count = pair.shape[1]
    named = (pair[0:1] == expert) | (pair[1:2] == expert)
    named = jnp.broadcast_to(jnp.where(named, 1.0, 0.0), (capacity, token_count))
    rank = dot(named.astype(BF16), earlier)
    slot = lax.broadcasted_iota(jnp.int32, (capacity, token_count), 0).astype(F32)
    return jnp.where(rank == slot, named, 0.0).astype(BF16)


ROUTE_ROWS = 16


def cut_columns(rows, pair, group, targets, groups, block):
    def end_of(index):
        return jnp.where(index < groups // 2, 0, groups - 1)

    token_count, width = rows.shape
    lines = token_count + ROUTE_ROWS
    if block % 128:
        wide = -(-block // 128) * 128

        def tail(columns):
            return jnp.pad(pair.astype(BF16), ((0, ROUTE_ROWS - 2), (0, columns - token_count)))

        def cut(index):
            return jnp.concatenate([cut_padded(rows, [index], block, wide), tail(wide)], axis=0)

        return [jnp.concatenate([rows, tail(width)], axis=0)] + [
            jnp.concatenate([cut(t)] + ([cut(end_of(t))] if k else []), axis=1) for k, t in enumerate(targets)
        ]
    scalars = targets + [end_of(t) for t in targets[1:]]
    count = len(targets)

    def body(s, ins, outs):
        held = jnp.concatenate([ins[0][...].astype(F32), jnp.zeros((ROUTE_ROWS - 2, token_count), F32)], axis=0)
        for i, o in zip(ins[1:], outs):
            o[:token_count] = i[...]
            o[token_count:] = jnp.zeros((ROUTE_ROWS, block), BF16)
            o[token_count:, :token_count] = held.astype(BF16)

    def from_block(k):
        if k == 0:
            return lambda j, s: (0, s[0])
        return lambda j, s: (0, jnp.where(j == 0, s[k], s[count + k - 1]))

    return call(
        body,
        "cut_columns",
        scalars,
        [pair] + [rows] * (count + 1),
        [whole(pair.shape), pl.BlockSpec((token_count, block), lambda j, s: (0, j))]
        + [pl.BlockSpec((token_count, block), from_block(k)) for k in range(count)],
        [((lines, width), BF16)] + [((lines, block * (1 if k == 0 else 2)), BF16) for k in range(count)],
        [pl.BlockSpec((lines, block), lambda j, s: (0, j))]
        + [
            pl.BlockSpec(
                (lines, block), (lambda j, s: (0, 0)) if k == 0 else (lambda j, s: (0, jnp.minimum(j, 1)))
            )
            for k in range(count)
        ],
        (groups,),
    )


def cut_padded(rows, indices, block, wide):
    pieces = [lax.dynamic_slice_in_dim(rows, i * block, block, axis=1) for i in indices]
    return jnp.concatenate([jnp.pad(p, ((0, 0), (0, wide - block))) for p in pieces], axis=1)


def join_columns(pieces, after=()):
    lines = pieces[0][0].shape[0]
    total = sum(size for _, _, size in pieces)

    def body(s, ins, outs):
        at = 0
        for ref, (_, first, size) in zip(ins, pieces):
            outs[0][:, at : at + size] = ref[...]
            at += size

    return call(
        body,
        "join_columns",
        [jnp.int32(0)],
        [array for array, _, _ in pieces],
        [pl.BlockSpec((lines, size), lambda j, s, c=first // size: (0, c)) for _, first, size in pieces],
        [((lines, total), BF16)],
        [whole((lines, total))],
        (1,),
        after=after,
    )[0]


def forward(expert, places, rows, upstream, gate_w, up_w, up_parts, first=None, after=()):
    sources = len(rows)
    lines, width = rows[0].shape
    token_count = lines - ROUTE_ROWS
    slots, hidden = upstream.shape
    capacity = slots // len(places)
    skip = 0 if first is None else len(places) - sources
    used = places[skip : skip + sources]
    step = 256 if hidden % 256 == 0 else hidden
    count = sources * capacity
    lead = skip * capacity
    spans, at = [], 0
    for size in up_parts:
        spans.append((at // step, (at + size) // step))
        at += size

    def body(s, ins, refs):
        tok = ins[:sources]
        up_ref, wg, wu = ins[sources : sources + 3]
        gate_out, up_outs, received = refs[0], refs[1:-1], refs[-1]
        j = pl.program_id(0)

        @pl.when(pl.program_id(0) == 0)
        def _():
            earlier = earlier_mask(token_count)
            for r in range(sources):
                mark = slot_marks(pair_in(tok[r], token_count), s[0], capacity, earlier)
                received[r * capacity : (r + 1) * capacity] = dot(mark, tok[r][:token_count]).astype(BF16)

        gate = dot(received[...], wg[...])
        up = dot(received[...], wu[...])
        for r in range(sources):
            here = slice(r * capacity, (r + 1) * capacity)
            g = gate[here]
            h = up_ref[pl.ds(pl.multiple_of(s[1 + r] * capacity, 16), capacity), :].astype(F32)
            sig = jax.nn.sigmoid(g)
            gate_out[here] = (h * up[here] * sig * (1.0 + g * (1.0 - sig))).astype(BF16)
            up_grad = (h * g * sig).astype(BF16)
            for (low, high), out in zip(spans, up_outs):

                @pl.when((j >= low) & (j < high))
                def _():
                    out[lead + r * capacity : lead + (r + 1) * capacity] = up_grad

        if first is not None:
            for (low, high), out in zip(spans, up_outs):

                @pl.when((j >= low) & (j < high))
                def _():
                    out[:lead] = ins[sources + 3][...]

    ins = list(rows) + [upstream, gate_w, up_w]
    specs = [whole((lines, width))] * sources
    specs += [pl.BlockSpec((slots, step), lambda j, s: (0, j))]
    specs += [pl.BlockSpec((width, step), lambda j, s: (0, j))] * 2
    if first is not None:
        ins.append(first)
        specs.append(pl.BlockSpec((lead, step), lambda j, s: (0, j)))
    return call(
        body,
        "forward_first" if first is None else "forward_rest",
        [expert] + used,
        ins,
        specs,
        [((count, hidden), BF16)] + [((lead + count, size), BF16) for size in up_parts],
        [pl.BlockSpec((count, step), lambda j, s: (0, j))]
        + [
            pl.BlockSpec((lead + count, step), lambda j, s, a=low, b=high: (0, jnp.clip(j - a, 0, b - a - 1)))
            for low, high in spans
        ],
        (hidden // step,),
        scratch=[pltpu.VMEM((count, width), BF16)],
        after=after,
        vmem=60,
    )


def halves_of(width):
    step = 512 if width % 512 == 0 else 128
    steps = width // step
    return step, steps, (steps + 1) // 2


def slot_gradients(places, gate, ups, gate_w, up_w, near=None, after=()):
    width, hidden = gate_w.shape
    count = gate.shape[0]
    skip = 0 if near is None else near.shape[0]
    slots = skip + count
    capacity = slots // len(places) if skip else count // 2
    step, steps, lead = halves_of(width)

    def body(s, ins, outs):
        j = pl.program_id(0)
        wg, wu = ins[0], ins[1]
        across = ((1,), (1,))
        total = dot(ins[2][...], wg[...], across)
        at = 0
        for g in ins[3 : 3 + len(ups)]:
            size = g.shape[1]
            total = total + dot(g[skip:], wu[:, at : at + size], across)
            at += size
        total = total.astype(BF16)
        if near is None:
            outs[0][...] = total
            return

        def put(out):
            for r in range(len(places)):
                at = pl.ds(pl.multiple_of(s[r] * capacity, 16), capacity)
                if r < 2:
                    out[at, :] = ins[-1][r * capacity : (r + 1) * capacity]
                else:
                    out[at, :] = total[(r - 2) * capacity : (r - 1) * capacity]

        @pl.when(j < lead)
        def _():
            put(outs[0])

        @pl.when(j >= lead)
        def _():
            put(outs[1])

    ins = [gate_w, up_w, gate] + list(ups)
    specs = [pl.BlockSpec((step, hidden), lambda j, s: (j, 0))] * 2 + [whole(g.shape) for g in ins[2:]]
    if near is None:
        outs = [((slots, width), BF16)]
        out_specs = [pl.BlockSpec((slots, step), lambda j, s: (0, j))]
    else:
        ins.append(near)
        specs.append(pl.BlockSpec((skip, step), lambda j, s: (0, j)))
        outs = [((slots, lead * step), BF16), ((slots, width - lead * step), BF16)]
        out_specs = [
            pl.BlockSpec((slots, step), lambda j, s: (0, jnp.minimum(j, lead - 1))),
            pl.BlockSpec((slots, step), lambda j, s: (0, jnp.maximum(j - lead, 0))),
        ]
    out = call(
        body,
        "near_gradients" if near is None else "slot_gradients",
        places,
        ins,
        specs,
        outs,
        out_specs,
        (steps,),
        after=after,
        vmem=60,
    )
    return out[0] if near is None else out


def combine(pair, returned, experts, after=()):
    token_count = pair.shape[1]
    slots, width = returned.shape
    capacity = slots // experts
    step = 512 if width % 512 == 0 else 128

    def body(s, ins, refs):
        marks = refs[-1]

        @pl.when(pl.program_id(0) == 0)
        def _():
            earlier = earlier_mask(token_count)
            for r in range(experts):
                marks[r * capacity : (r + 1) * capacity] = slot_marks(ins[0][...], r, capacity, earlier)

        refs[0][...] = dot(marks[...], ins[1][...], ((0,), (0,))).astype(BF16)

    return call(
        body,
        "combine",
        [jnp.int32(0)],
        [pair, returned],
        [whole(pair.shape), pl.BlockSpec((slots, step), lambda j, s: (0, j))],
        [((token_count, width), BF16)],
        [pl.BlockSpec((token_count, step), lambda j, s: (0, j))],
        (width // step,),
        scratch=[pltpu.VMEM((slots, token_count), BF16)],
        after=after,
    )[0]


def pick_rows(expert, blocks, rows, capacity, block, routes=None, after=()):
    sources = len(rows)
    lines = rows[0].shape[0]
    token_count = lines - ROUTE_ROWS
    count = len(blocks)

    def body(s, ins, outs):
        earlier = earlier_mask(token_count)
        picked = []
        for r in range(sources):
            pair = pair_in(ins[r], token_count) if routes is None else ins[sources + r][...]
            pair = pair.astype(F32).astype(jnp.int32)
            mark = slot_marks(pair, s[0], capacity, earlier)
            picked.append(dot(mark, ins[r][:token_count]))
        outs[0][...] = jnp.concatenate(picked, axis=0).astype(BF16).T

    ins, specs = list(rows), []
    for r in range(sources):
        specs.append(pl.BlockSpec((lines, block), lambda j, s: (0, s[1 + j])))
    if routes is not None:
        ins += list(routes)
        specs += [
            pl.BlockSpec((ROUTE_ROWS, token_count), lambda j, s: (token_count // ROUTE_ROWS, 0)) for _ in routes
        ]
    return call(
        body,
        "pick_rows",
        [expert] + list(blocks),
        ins,
        specs,
        [((count * block, sources * capacity), BF16)],
        [pl.BlockSpec((block, sources * capacity), lambda j, s: (j, 0))],
        (count,),
        after=after,
    )[0]


def products(terms, block, part, dtype, name, extras=(), total=None, after=(), vmem=28):
    slots = terms[0][0].shape[1]
    split = 2 if block % 32 == 0 else 1
    lines = block // split

    def body(s, ins, outs):
        at, result = len(terms), None
        for k, (_, _, parts) in enumerate(terms):
            row = 0
            for _ in parts:
                g = ins[at]
                new = dot(ins[k][:, row : row + g.shape[0]] if len(parts) > 1 else ins[k][...], g[...])
                result = new if result is None else result + new
                row += g.shape[0]
                at += 1
        if extras:
            result = result + jnp.concatenate([e[...].astype(F32) for e in ins[at:]], axis=1)
        outs[0][...] = result.astype(dtype)

    ins = [p for p, _, _ in terms]
    specs = [pl.BlockSpec((lines, slots), lambda j, s, i=i: (i * split + j, 0)) for _, i, _ in terms]
    for _, _, parts in terms:
        for array, column in parts:
            ins.append(array)
            specs.append(pl.BlockSpec((array.shape[0], part), lambda j, s, c=column: (0, c)))
    for e in extras:
        ins.append(e)
        specs.append(pl.BlockSpec((lines, e.shape[1]), lambda j, s: (j, 0)))
    return call(
        body,
        name,
        [jnp.int32(0)],
        ins,
        specs,
        [((block, total or part), dtype)],
        [pl.BlockSpec((lines, part), lambda j, s: (j, 0))],
        (split,),
        after=after,
        vmem=vmem,
    )[0]


def finish(own, extra, target, place, total, after=()):
    block, part = own.shape
    ins = [own, extra]
    specs = [whole((block, part))] * 2
    if target is not None:
        ins.append(target)
        specs.append(pl.BlockSpec(memory_space=pl.ANY))

    def body(s, refs, outs):
        outs[0][...] = (refs[0][...] + refs[1][...].astype(F32)).astype(BF16)

    return call(
        body,
        "finish",
        [jnp.int32(0)],
        ins,
        specs,
        [((block, total), BF16)],
        [pl.BlockSpec((block, part), lambda j, s: (0, place))],
        (1,),
        after=after,
        aliases={3: 0} if target is not None else None,
    )[0]


def tied(value, *others):
    return lax.optimization_barrier((value,) + others)[0]


def shards(tokens, routes, hidden_grad, w_gate, w_up):
    groups = lax.axis_size("dp")
    experts = lax.axis_size("expert")
    sections = lax.axis_size("section")
    group = lax.axis_index("dp")
    expert = lax.axis_index("expert")
    rows = tokens[0]
    token_count, width = rows.shape
    slots = hidden_grad.shape[3]
    capacity = slots // experts
    hidden = w_gate.shape[3]
    block = width // groups
    gate_w = w_gate[0, 0]
    up_w = w_up[0, 0]
    upstream = hidden_grad[0, 0, 0]
    sets = grouped_pairs(groups)
    up_parts = [hidden // 2, hidden // 2]
    wide = -(-block // 128) * 128
    own_blocks = [group, jnp.where(group < groups // 2, 0, groups - 1)]

    def swap(value):
        return lax.ppermute(value, "expert", [(s, s ^ 1) for s in range(experts)])

    def shift(value, by):
        return lax.ppermute(value, "expert", [(s, (s + 2 * by) % experts) for s in range(experts)])

    def over_groups(value, pairs):
        return lax.ppermute(value, "dp", pairs)

    def to_sources(value):
        back = lax.all_to_all(
            value.reshape(experts, capacity, value.shape[1]), "expert", split_axis=0, concat_axis=0, tiled=True
        )
        return back.reshape(value.shape)

    def passed_on(value):
        return lax.ppermute(value, "section", [(s, (s - 1) % sections) for s in range(sections)])

    def to_ends(value):
        return lax.ppermute(value, "dp", [(1, 0), (groups - 2, groups - 1)])

    chips = range(1, experts // 2)
    places = [jnp.bitwise_xor((expert - 2 * (r // 2)) % experts, r % 2) for r in range(experts)]
    targets = [target_in(pairs, group) for pairs in sets]
    order = list(range(1, len(sets))) + [0]

    pair = routes[0].T
    own, *cut = cut_columns(rows, pair, group, targets, groups, block)
    far_even = [shift(own, by) for by in chips]
    others = {k: over_groups(cut[k], sets[k]) for k in order}
    partner = swap(own)
    near_gate, near_up = forward(expert, places, [own, partner], upstream, gate_w, up_w, [hidden])
    near_back = slot_gradients(places, near_gate, [near_up], gate_w, up_w, after=[near_gate])
    epoch = [others[k] for k in order] + far_even + [near_back]

    near_sent = {k: over_groups(tied(near_gate, *epoch), sets[k]) for k in order}
    far = []
    for value in far_even:
        far += [value, swap(tied(value, *epoch))]
    end_columns = join_columns([(others[k], wide, wide) for k in range(1, len(sets))], after=epoch)
    end_far = [shift(end_columns, by) for by in chips]
    far_gate, *ups = forward(
        expert, places, far, upstream, gate_w, up_w, up_parts, first=near_up, after=[end_columns]
    )
    own_columns = [own, partner] + far
    own_lines = own_columns
    if wide != block:
        own_columns = [cut_padded(v, own_blocks, block, wide) for v in own_columns]
        own_blocks = [jnp.int32(0), jnp.int32(1)]
    own_picked = pick_rows(
        expert, own_blocks, own_columns, capacity, wide, routes=own_lines, after=[far_gate]
    )
    own_part = join_columns([(others[k], 0, wide) for k in range(len(sets))], after=[own_picked])
    epoch = [near_sent[k] for k in order] + [own_part]

    far_sent = {k: over_groups(tied(far_gate, *epoch), sets[k]) for k in order}
    first_back, second_back = slot_gradients(
        places, far_gate, ups, gate_w, up_w, near=near_back, after=epoch
    )
    first_back = to_sources(first_back)
    end_rows = []
    for value in [end_columns] + end_far:
        end_rows += [value, swap(tied(value, *epoch))]
    column_far = [shift(tied(own_part, *epoch), by) for by in chips]
    end_picked = pick_rows(
        expert, [jnp.int32(k) for k in range(len(sets) - 1)], end_rows, capacity, wide, after=[second_back]
    )
    epoch = [far_sent[k] for k in order] + [end_picked]

    def parts_of(c):
        if c == 0:
            out = [[(near_gate, c), (far_gate, c)]]
            out += [[(near_sent[k], c), (far_sent[k], c)] for k in range(len(sets))]
        else:
            out = [[(ups[c - 1], 0)]] + [[(up_sent[c - 1][k], 0)] for k in range(len(sets))]
        return out

    def for_end(c, after):
        parts = parts_of(c)
        part = up_parts[c - 1] if c else hidden
        terms = [(own_picked, 1, parts[0])]
        terms += [(end_picked, k - 1, parts[1 + k]) for k in range(1, len(sets))]
        return products(terms, wide, part, BF16, "for_end", after=after, vmem=60 if c else 28)

    def for_own(c, part, dtype, after, extras=(), total=None):
        parts = parts_of(c)
        terms = [(own_picked, 0, parts[0])]
        terms += [(picked, k, parts[1 + k]) for k in range(len(sets))]
        return products(terms, wide, part, dtype, "for_own", extras=extras, total=total, after=after, vmem=60 if c == 0 else 28)

    up_sent = []

    def send_up(c):
        up_sent.append({k: over_groups(tied(ups[c], *epoch), sets[k]) for k in order})
        return [up_sent[c][k] for k in order]

    arriving = send_up(0)
    column_rows = []
    for value in [own_part] + column_far:
        column_rows += [value, swap(tied(value, *epoch))]
    end0 = for_end(0, epoch)
    extra0 = to_ends(end0)
    picked = pick_rows(
        expert, [jnp.int32(k) for k in range(len(sets))], column_rows, capacity, wide, after=[end0]
    )
    epoch = arriving + [picked, first_back]

    arriving = send_up(1)
    second_back = to_sources(tied(second_back, *epoch))
    end1 = for_end(1, epoch)
    extra1 = to_ends(end1)
    first_tok = combine(pair, first_back, experts, after=[end1])
    first_passed = passed_on(first_tok)
    gate = for_own(0, hidden, BF16, [first_tok], extras=[extra0])
    epoch = arriving + [gate]

    end2 = for_end(2, epoch)
    extra2 = to_ends(end2)
    second_tok = combine(pair, second_back, experts, after=[end2])
    second_passed = passed_on(second_tok)
    up0 = for_own(1, up_parts[0], BF16, [second_tok], extras=[extra1], total=hidden)
    own2 = for_own(2, up_parts[1], F32, [up0])
    passed = jnp.concatenate([tied(first_passed, own2), second_passed], axis=1)
    up1 = finish(own2, extra2, up0, up_parts[0] // up_parts[1], hidden)
    return (passed[None], gate[None, None, :block], up1[None, None, :block])


def solution(mesh):
    placed = (
        P("section", ("dp", "expert"), None),
        P("section", ("dp", "expert"), None),
        P("section", "dp", "expert", None, None),
        P("section", "expert", None, None),
        P("section", "expert", None, None),
    )
    return jax.shard_map(
        shards,
        mesh=mesh,
        in_specs=placed,
        out_specs=(
            P("section", ("dp", "expert"), None),
            P("section", "expert", "dp", None),
            P("section", "expert", "dp", None),
        ),
        check_vma=False,
    )
```

```python
import jax
import jax.numpy as jnp
from jax import lax
from jax.experimental import pallas as pl
from jax.experimental.pallas import tpu as pltpu
from jax.sharding import PartitionSpec as P

BF16 = jnp.bfloat16
F32 = jnp.float32
MIB = 1024 * 1024


def dot(a, b, contract=((1,), (0,))):
    return lax.dot_general(a, b, (contract, ((), ())), preferred_element_type=F32)


def grouped_pairs(count):
    first, last = 0, count - 1
    sets = []
    inner = range(1, last)
    for j, i in sorted(((j, i) for j in inner for i in inner if j != i), key=lambda p: (abs(p[0] - p[1]), p)):
        for chosen in sets:
            if all(j != a and i != b for a, b in chosen):
                chosen.append((j, i))
                break
        else:
            sets.append([(j, i)])
    out = [[(first, 1), (last, last - 1)]]
    for chosen in sets:
        out.append(chosen)
        out.append([({1: first, last - 1: last}[j], i) for j, i in chosen if j in (1, last - 1)])
    return out


def target_in(pairs, index):
    found = jnp.int32(0)
    for source, target in pairs:
        found = jnp.where(index == source, target, found)
    return found


def call(body, name, scalars, ins, in_specs, outs, out_specs, grid, scratch=(), after=(), aliases=None, vmem=28):
    count, skip = len(ins), len(after)

    def kernel(scalar_ref, *refs):
        body(scalar_ref, refs[:count], refs[count + skip :])

    return pl.pallas_call(
        kernel,
        name=name,
        out_shape=[jax.ShapeDtypeStruct(shape, dtype) for shape, dtype in outs],
        grid_spec=pltpu.PrefetchScalarGridSpec(
            num_scalar_prefetch=1,
            grid=grid,
            in_specs=list(in_specs) + [pl.BlockSpec(memory_space=pl.ANY)] * skip,
            out_specs=list(out_specs),
            scratch_shapes=list(scratch),
        ),
        input_output_aliases=aliases or {},
        compiler_params=pltpu.CompilerParams(
            dimension_semantics=("arbitrary",) * len(grid), vmem_limit_bytes=vmem * MIB
        ),
        cost_estimate=pl.CostEstimate(flops=1, bytes_accessed=1, transcendentals=0),
    )(jnp.stack(scalars).astype(jnp.int32), *ins, *after)


def whole(shape):
    return pl.BlockSpec(shape, lambda j, s: (0,) * len(shape))


def earlier_mask(token_count):
    first = lax.broadcasted_iota(jnp.int32, (token_count, token_count), 0)
    second = lax.broadcasted_iota(jnp.int32, (token_count, token_count), 1)
    return jnp.where(first < second, 1.0, 0.0).astype(BF16)


def pair_in(ref, token_count):
    return ref[token_count:, :token_count].astype(F32).astype(jnp.int32)


def slot_marks(pair, expert, capacity, earlier):
    token_count = pair.shape[1]
    named = (pair[0:1] == expert) | (pair[1:2] == expert)
    named = jnp.broadcast_to(jnp.where(named, 1.0, 0.0), (capacity, token_count))
    rank = dot(named.astype(BF16), earlier)
    slot = lax.broadcasted_iota(jnp.int32, (capacity, token_count), 0).astype(F32)
    return jnp.where(rank == slot, named, 0.0).astype(BF16)


ROUTE_ROWS = 16


def cut_columns(rows, pair, group, targets, groups, block):
    def end_of(index):
        return jnp.where(index < groups // 2, 0, groups - 1)

    token_count, width = rows.shape
    lines = token_count + ROUTE_ROWS
    if block % 128:
        wide = -(-block // 128) * 128

        def tail(columns):
            return jnp.pad(pair.astype(BF16), ((0, ROUTE_ROWS - 2), (0, columns - token_count)))

        def cut(index):
            return jnp.concatenate([cut_padded(rows, [index], block, wide), tail(wide)], axis=0)

        return [jnp.concatenate([rows, tail(width)], axis=0)] + [
            jnp.concatenate([cut(t)] + ([cut(end_of(t))] if k else []), axis=1) for k, t in enumerate(targets)
        ]
    scalars = targets + [end_of(t) for t in targets[1:]]
    count = len(targets)

    def body(s, ins, outs):
        held = jnp.concatenate([ins[0][...].astype(F32), jnp.zeros((ROUTE_ROWS - 2, token_count), F32)], axis=0)
        for i, o in zip(ins[1:], outs):
            o[:token_count] = i[...]
            o[token_count:] = jnp.zeros((ROUTE_ROWS, block), BF16)
            o[token_count:, :token_count] = held.astype(BF16)

    def from_block(k):
        if k == 0:
            return lambda j, s: (0, s[0])
        return lambda j, s: (0, jnp.where(j == 0, s[k], s[count + k - 1]))

    return call(
        body,
        "cut_columns",
        scalars,
        [pair] + [rows] * (count + 1),
        [whole(pair.shape), pl.BlockSpec((token_count, block), lambda j, s: (0, j))]
        + [pl.BlockSpec((token_count, block), from_block(k)) for k in range(count)],
        [((lines, width), BF16)] + [((lines, block * (1 if k == 0 else 2)), BF16) for k in range(count)],
        [pl.BlockSpec((lines, block), lambda j, s: (0, j))]
        + [
            pl.BlockSpec(
                (lines, block), (lambda j, s: (0, 0)) if k == 0 else (lambda j, s: (0, jnp.minimum(j, 1)))
            )
            for k in range(count)
        ],
        (groups,),
    )


def cut_padded(rows, indices, block, wide):
    pieces = [lax.dynamic_slice_in_dim(rows, i * block, block, axis=1) for i in indices]
    return jnp.concatenate([jnp.pad(p, ((0, 0), (0, wide - block))) for p in pieces], axis=1)


def join_columns(pieces, after=()):
    lines = pieces[0][0].shape[0]
    total = sum(size for _, _, size in pieces)

    def body(s, ins, outs):
        at = 0
        for ref, (_, first, size) in zip(ins, pieces):
            outs[0][:, at : at + size] = ref[...]
            at += size

    return call(
        body,
        "join_columns",
        [jnp.int32(0)],
        [array for array, _, _ in pieces],
        [pl.BlockSpec((lines, size), lambda j, s, c=first // size: (0, c)) for _, first, size in pieces],
        [((lines, total), BF16)],
        [whole((lines, total))],
        (1,),
        after=after,
    )[0]


def forward(expert, places, rows, upstream, gate_w, up_w, up_parts, first=None, after=()):
    sources = len(rows)
    lines, width = rows[0].shape
    token_count = lines - ROUTE_ROWS
    slots, hidden = upstream.shape
    capacity = slots // len(places)
    skip = 0 if first is None else len(places) - sources
    used = places[skip : skip + sources]
    step = 256 if hidden % 256 == 0 else hidden
    count = sources * capacity
    lead = skip * capacity
    spans, at = [], 0
    for size in up_parts:
        spans.append((at // step, (at + size) // step))
        at += size

    def body(s, ins, refs):
        tok = ins[:sources]
        up_ref, wg, wu = ins[sources : sources + 3]
        gate_out, up_outs, received = refs[0], refs[1:-1], refs[-1]
        j = pl.program_id(0)

        @pl.when(pl.program_id(0) == 0)
        def _():
            earlier = earlier_mask(token_count)
            for r in range(sources):
                mark = slot_marks(pair_in(tok[r], token_count), s[0], capacity, earlier)
                received[r * capacity : (r + 1) * capacity] = dot(mark, tok[r][:token_count]).astype(BF16)

        gate = dot(received[...], wg[...])
        up = dot(received[...], wu[...])
        for r in range(sources):
            here = slice(r * capacity, (r + 1) * capacity)
            g = gate[here]
            h = up_ref[pl.ds(pl.multiple_of(s[1 + r] * capacity, 16), capacity), :].astype(F32)
            sig = jax.nn.sigmoid(g)
            gate_out[here] = (h * up[here] * sig * (1.0 + g * (1.0 - sig))).astype(BF16)
            up_grad = (h * g * sig).astype(BF16)
            for (low, high), out in zip(spans, up_outs):

                @pl.when((j >= low) & (j < high))
                def _():
                    out[lead + r * capacity : lead + (r + 1) * capacity] = up_grad

        if first is not None:
            for (low, high), out in zip(spans, up_outs):

                @pl.when((j >= low) & (j < high))
                def _():
                    out[:lead] = ins[sources + 3][...]

    ins = list(rows) + [upstream, gate_w, up_w]
    specs = [whole((lines, width))] * sources
    specs += [pl.BlockSpec((slots, step), lambda j, s: (0, j))]
    specs += [pl.BlockSpec((width, step), lambda j, s: (0, j))] * 2
    if first is not None:
        ins.append(first)
        specs.append(pl.BlockSpec((lead, step), lambda j, s: (0, j)))
    return call(
        body,
        "forward_first" if first is None else "forward_rest",
        [expert] + used,
        ins,
        specs,
        [((count, hidden), BF16)] + [((lead + count, size), BF16) for size in up_parts],
        [pl.BlockSpec((count, step), lambda j, s: (0, j))]
        + [
            pl.BlockSpec((lead + count, step), lambda j, s, a=low, b=high: (0, jnp.clip(j - a, 0, b - a - 1)))
            for low, high in spans
        ],
        (hidden // step,),
        scratch=[pltpu.VMEM((count, width), BF16)],
        after=after,
        vmem=60,
    )


def halves_of(width):
    step = 512 if width % 512 == 0 else 128
    steps = width // step
    return step, steps, (steps + 1) // 2


def slot_gradients(places, gate, ups, gate_w, up_w, near=None, after=()):
    width, hidden = gate_w.shape
    count = gate.shape[0]
    skip = 0 if near is None else near.shape[0]
    slots = skip + count
    capacity = slots // len(places) if skip else count // 2
    step, steps, lead = halves_of(width)

    def body(s, ins, outs):
        j = pl.program_id(0)
        wg, wu = ins[0], ins[1]
        across = ((1,), (1,))
        total = dot(ins[2][...], wg[...], across)
        at = 0
        for g in ins[3 : 3 + len(ups)]:
            size = g.shape[1]
            total = total + dot(g[skip:], wu[:, at : at + size], across)
            at += size
        total = total.astype(BF16)
        if near is None:
            outs[0][...] = total
            return

        def put(out):
            for r in range(len(places)):
                at = pl.ds(pl.multiple_of(s[r] * capacity, 16), capacity)
                if r < 2:
                    out[at, :] = ins[-1][r * capacity : (r + 1) * capacity]
                else:
                    out[at, :] = total[(r - 2) * capacity : (r - 1) * capacity]

        @pl.when(j < lead)
        def _():
            put(outs[0])

        @pl.when(j >= lead)
        def _():
            put(outs[1])

    ins = [gate_w, up_w, gate] + list(ups)
    specs = [pl.BlockSpec((step, hidden), lambda j, s: (j, 0))] * 2 + [whole(g.shape) for g in ins[2:]]
    if near is None:
        outs = [((slots, width), BF16)]
        out_specs = [pl.BlockSpec((slots, step), lambda j, s: (0, j))]
    else:
        ins.append(near)
        specs.append(pl.BlockSpec((skip, step), lambda j, s: (0, j)))
        outs = [((slots, lead * step), BF16), ((slots, width - lead * step), BF16)]
        out_specs = [
            pl.BlockSpec((slots, step), lambda j, s: (0, jnp.minimum(j, lead - 1))),
            pl.BlockSpec((slots, step), lambda j, s: (0, jnp.maximum(j - lead, 0))),
        ]
    out = call(
        body,
        "near_gradients" if near is None else "slot_gradients",
        places,
        ins,
        specs,
        outs,
        out_specs,
        (steps,),
        after=after,
        vmem=60,
    )
    return out[0] if near is None else out


def combine(pair, returned, experts, after=()):
    token_count = pair.shape[1]
    slots, width = returned.shape
    capacity = slots // experts
    step = 512 if width % 512 == 0 else 128

    def body(s, ins, refs):
        marks = refs[-1]

        @pl.when(pl.program_id(0) == 0)
        def _():
            earlier = earlier_mask(token_count)
            for r in range(experts):
                marks[r * capacity : (r + 1) * capacity] = slot_marks(ins[0][...], r, capacity, earlier)

        refs[0][...] = dot(marks[...], ins[1][...], ((0,), (0,))).astype(BF16)

    return call(
        body,
        "combine",
        [jnp.int32(0)],
        [pair, returned],
        [whole(pair.shape), pl.BlockSpec((slots, step), lambda j, s: (0, j))],
        [((token_count, width), BF16)],
        [pl.BlockSpec((token_count, step), lambda j, s: (0, j))],
        (width // step,),
        scratch=[pltpu.VMEM((slots, token_count), BF16)],
        after=after,
    )[0]


def pick_rows(expert, blocks, rows, capacity, block, routes=None, after=()):
    sources = len(rows)
    lines = rows[0].shape[0]
    token_count = lines - ROUTE_ROWS
    count = len(blocks)

    def body(s, ins, outs):
        earlier = earlier_mask(token_count)
        picked = []
        for r in range(sources):
            pair = pair_in(ins[r], token_count) if routes is None else ins[sources + r][...]
            pair = pair.astype(F32).astype(jnp.int32)
            mark = slot_marks(pair, s[0], capacity, earlier)
            picked.append(dot(mark, ins[r][:token_count]))
        outs[0][...] = jnp.concatenate(picked, axis=0).astype(BF16).T

    ins, specs = list(rows), []
    for r in range(sources):
        specs.append(pl.BlockSpec((lines, block), lambda j, s: (0, s[1 + j])))
    if routes is not None:
        ins += list(routes)
        specs += [
            pl.BlockSpec((ROUTE_ROWS, token_count), lambda j, s: (token_count // ROUTE_ROWS, 0)) for _ in routes
        ]
    return call(
        body,
        "pick_rows",
        [expert] + list(blocks),
        ins,
        specs,
        [((count * block, sources * capacity), BF16)],
        [pl.BlockSpec((block, sources * capacity), lambda j, s: (j, 0))],
        (count,),
        after=after,
    )[0]


def products(terms, block, part, dtype, name, extras=(), total=None, after=(), vmem=28):
    slots = terms[0][0].shape[1]
    split = 2 if block % 32 == 0 else 1
    lines = block // split

    count = len(terms)
    pieces = sum(len(parts) for _, _, parts in terms)

    def body(s, ins, outs):
        left = jnp.concatenate([p[...] for p in ins[:count]], axis=1)
        right = jnp.concatenate([g[...] for g in ins[count : count + pieces]], axis=0)
        result = dot(left, right)
        if extras:
            result = result + jnp.concatenate([e[...].astype(F32) for e in ins[count + pieces :]], axis=1)
        outs[0][...] = result.astype(dtype)

    ins = [p for p, _, _ in terms]
    specs = [pl.BlockSpec((lines, slots), lambda j, s, i=i: (i * split + j, 0)) for _, i, _ in terms]
    for _, _, parts in terms:
        for array, column in parts:
            ins.append(array)
            specs.append(pl.BlockSpec((array.shape[0], part), lambda j, s, c=column: (0, c)))
    for e in extras:
        ins.append(e)
        specs.append(pl.BlockSpec((lines, e.shape[1]), lambda j, s: (j, 0)))
    return call(
        body,
        name,
        [jnp.int32(0)],
        ins,
        specs,
        [((block, total or part), dtype)],
        [pl.BlockSpec((lines, part), lambda j, s: (j, 0))],
        (split,),
        after=after,
        vmem=vmem,
    )[0]


def finish(own, extra, target, place, total, after=()):
    block, part = own.shape
    ins = [own, extra]
    specs = [whole((block, part))] * 2
    if target is not None:
        ins.append(target)
        specs.append(pl.BlockSpec(memory_space=pl.ANY))

    def body(s, refs, outs):
        outs[0][...] = (refs[0][...] + refs[1][...].astype(F32)).astype(BF16)

    return call(
        body,
        "finish",
        [jnp.int32(0)],
        ins,
        specs,
        [((block, total), BF16)],
        [pl.BlockSpec((block, part), lambda j, s: (0, place))],
        (1,),
        after=after,
        aliases={3: 0} if target is not None else None,
    )[0]


def tied(value, *others):
    return lax.optimization_barrier((value,) + others)[0]


def shards(tokens, routes, hidden_grad, w_gate, w_up):
    groups = lax.axis_size("dp")
    experts = lax.axis_size("expert")
    sections = lax.axis_size("section")
    group = lax.axis_index("dp")
    expert = lax.axis_index("expert")
    rows = tokens[0]
    token_count, width = rows.shape
    slots = hidden_grad.shape[3]
    capacity = slots // experts
    hidden = w_gate.shape[3]
    block = width // groups
    gate_w = w_gate[0, 0]
    up_w = w_up[0, 0]
    upstream = hidden_grad[0, 0, 0]
    sets = grouped_pairs(groups)
    up_parts = [hidden // 2, hidden // 2]
    wide = -(-block // 128) * 128
    own_blocks = [group, jnp.where(group < groups // 2, 0, groups - 1)]

    def swap(value):
        return lax.ppermute(value, "expert", [(s, s ^ 1) for s in range(experts)])

    def shift(value, by):
        return lax.ppermute(value, "expert", [(s, (s + 2 * by) % experts) for s in range(experts)])

    def over_groups(value, pairs):
        return lax.ppermute(value, "dp", pairs)

    def to_sources(value):
        back = lax.all_to_all(
            value.reshape(experts, capacity, value.shape[1]), "expert", split_axis=0, concat_axis=0, tiled=True
        )
        return back.reshape(value.shape)

    def passed_on(value):
        return lax.ppermute(value, "section", [(s, (s - 1) % sections) for s in range(sections)])

    def to_ends(value):
        return lax.ppermute(value, "dp", [(1, 0), (groups - 2, groups - 1)])

    chips = range(1, experts // 2)
    places = [jnp.bitwise_xor((expert - 2 * (r // 2)) % experts, r % 2) for r in range(experts)]
    targets = [target_in(pairs, group) for pairs in sets]
    order = list(range(2, len(sets))) + [1, 0]

    pair = routes[0].T
    own, *cut = cut_columns(rows, pair, group, targets, groups, block)
    far_even = [shift(own, by) for by in chips]
    others = {k: over_groups(cut[k], sets[k]) for k in order}
    partner = swap(own)
    near_gate, near_up = forward(expert, places, [own, partner], upstream, gate_w, up_w, [hidden])
    near_back = slot_gradients(places, near_gate, [near_up], gate_w, up_w, after=[near_gate])
    epoch = [others[k] for k in order] + far_even + [near_back]

    near_sent = {k: over_groups(tied(near_gate, *epoch), sets[k]) for k in order}
    far = []
    for value in far_even:
        far += [value, swap(tied(value, *epoch))]
    end_columns = join_columns([(others[k], wide, wide) for k in range(1, len(sets))], after=epoch)
    end_far = [shift(end_columns, by) for by in chips]
    far_gate, *ups = forward(
        expert, places, far, upstream, gate_w, up_w, up_parts, first=near_up, after=[end_columns]
    )
    own_columns = [own, partner] + far
    own_lines = own_columns
    if wide != block:
        own_columns = [cut_padded(v, own_blocks, block, wide) for v in own_columns]
        own_blocks = [jnp.int32(0), jnp.int32(1)]
    own_picked = pick_rows(
        expert, own_blocks, own_columns, capacity, wide, routes=own_lines, after=[far_gate]
    )
    own_part = join_columns([(others[k], 0, wide) for k in range(len(sets))], after=[own_picked])
    epoch = [near_sent[k] for k in order] + [own_part]

    far_sent = {k: over_groups(tied(far_gate, *epoch), sets[k]) for k in order}
    first_back, second_back = slot_gradients(
        places, far_gate, ups, gate_w, up_w, near=near_back, after=epoch
    )
    first_back = to_sources(first_back)
    end_rows = []
    for value in [end_columns] + end_far:
        end_rows += [value, swap(tied(value, *epoch))]
    column_far = [shift(tied(own_part, *epoch), by) for by in chips]
    end_picked = pick_rows(
        expert, [jnp.int32(k) for k in range(len(sets) - 1)], end_rows, capacity, wide, after=[second_back]
    )
    epoch = [far_sent[k] for k in order] + [end_picked]

    def parts_of(c):
        if c == 0:
            out = [[(near_gate, c), (far_gate, c)]]
            out += [[(near_sent[k], c), (far_sent[k], c)] for k in range(len(sets))]
        else:
            out = [[(ups[c - 1], 0)]] + [[(up_sent[c - 1][k], 0)] for k in range(len(sets))]
        return out

    def for_end(c, after):
        parts = parts_of(c)
        part = up_parts[c - 1] if c else hidden
        terms = [(own_picked, 1, parts[0])]
        terms += [(end_picked, k - 1, parts[1 + k]) for k in reversed(range(1, len(sets)))]
        return products(terms, wide, part, BF16, "for_end", after=after, vmem=60)

    def for_own(c, part, dtype, after, extras=(), total=None):
        parts = parts_of(c)
        terms = [(own_picked, 0, parts[0])]
        terms += [(picked, k, parts[1 + k]) for k in reversed(range(len(sets)))]
        return products(terms, wide, part, dtype, "for_own", extras=extras, total=total, after=after, vmem=60)

    up_sent = []

    def send_up(c):
        up_sent.append({k: over_groups(tied(ups[c], *epoch), sets[k]) for k in order})
        return [up_sent[c][k] for k in order]

    arriving = send_up(0)
    column_rows = []
    for value in [own_part] + column_far:
        column_rows += [value, swap(tied(value, *epoch))]
    end0 = for_end(0, epoch)
    extra0 = to_ends(end0)
    picked = pick_rows(
        expert, [jnp.int32(k) for k in range(len(sets))], column_rows, capacity, wide, after=[end0]
    )
    epoch = arriving + [picked, first_back]

    arriving = send_up(1)
    second_back = to_sources(tied(second_back, *epoch))
    end1 = for_end(1, epoch)
    extra1 = to_ends(end1)
    first_tok = combine(pair, first_back, experts, after=[end1])
    first_passed = passed_on(first_tok)
    gate = for_own(0, hidden, BF16, [first_tok], extras=[extra0])
    epoch = arriving + [gate]

    end2 = for_end(2, epoch)
    extra2 = to_ends(end2)
    second_tok = combine(pair, second_back, experts, after=[end2])
    second_passed = passed_on(second_tok)
    up0 = for_own(1, up_parts[0], BF16, [second_tok], extras=[extra1], total=hidden)
    own2 = for_own(2, up_parts[1], F32, [up0])
    passed = jnp.concatenate([tied(first_passed, own2), second_passed], axis=1)
    up1 = finish(own2, extra2, up0, up_parts[0] // up_parts[1], hidden)
    return (passed[None], gate[None, None, :block], up1[None, None, :block])


def solution(mesh):
    placed = (
        P("section", ("dp", "expert"), None),
        P("section", ("dp", "expert"), None),
        P("section", "dp", "expert", None, None),
        P("section", "expert", None, None),
        P("section", "expert", None, None),
    )
    return jax.shard_map(
        shards,
        mesh=mesh,
        in_specs=placed,
        out_specs=(
            P("section", ("dp", "expert"), None),
            P("section", "expert", "dp", None),
            P("section", "expert", "dp", None),
        ),
        check_vma=False,
    )
```

```python
import jax
import jax.numpy as jnp
from jax import lax
from jax.experimental import pallas as pl
from jax.experimental.pallas import tpu as pltpu
from jax.sharding import PartitionSpec as P

BF16 = jnp.bfloat16
F32 = jnp.float32
MIB = 1024 * 1024


def dot(a, b, contract=((1,), (0,))):
    return lax.dot_general(a, b, (contract, ((), ())), preferred_element_type=F32)


def grouped_pairs(count):
    first, last = 0, count - 1
    sets = []
    inner = range(1, last)
    for j, i in sorted(((j, i) for j in inner for i in inner if j != i), key=lambda p: (abs(p[0] - p[1]), p)):
        for chosen in sets:
            if all(j != a and i != b for a, b in chosen):
                chosen.append((j, i))
                break
        else:
            sets.append([(j, i)])
    out = [[(first, 1), (last, last - 1)]]
    for chosen in sets:
        out.append(chosen)
        out.append([({1: first, last - 1: last}[j], i) for j, i in chosen if j in (1, last - 1)])
    return out


def target_in(pairs, index):
    found = jnp.int32(0)
    for source, target in pairs:
        found = jnp.where(index == source, target, found)
    return found


def call(body, name, scalars, ins, in_specs, outs, out_specs, grid, scratch=(), after=(), aliases=None, vmem=28):
    count, skip = len(ins), len(after)

    def kernel(scalar_ref, *refs):
        body(scalar_ref, refs[:count], refs[count + skip :])

    return pl.pallas_call(
        kernel,
        name=name,
        out_shape=[jax.ShapeDtypeStruct(shape, dtype) for shape, dtype in outs],
        grid_spec=pltpu.PrefetchScalarGridSpec(
            num_scalar_prefetch=1,
            grid=grid,
            in_specs=list(in_specs) + [pl.BlockSpec(memory_space=pl.ANY)] * skip,
            out_specs=list(out_specs),
            scratch_shapes=list(scratch),
        ),
        input_output_aliases=aliases or {},
        compiler_params=pltpu.CompilerParams(
            dimension_semantics=("arbitrary",) * len(grid), vmem_limit_bytes=vmem * MIB
        ),
        cost_estimate=pl.CostEstimate(flops=1, bytes_accessed=1, transcendentals=0),
    )(jnp.stack(scalars).astype(jnp.int32), *ins, *after)


def whole(shape):
    return pl.BlockSpec(shape, lambda j, s: (0,) * len(shape))


def earlier_mask(token_count):
    first = lax.broadcasted_iota(jnp.int32, (token_count, token_count), 0)
    second = lax.broadcasted_iota(jnp.int32, (token_count, token_count), 1)
    return jnp.where(first < second, 1.0, 0.0).astype(BF16)


def pair_in(ref, token_count):
    return ref[token_count:, :token_count].astype(F32).astype(jnp.int32)


def slot_marks(pair, expert, capacity, earlier):
    token_count = pair.shape[1]
    named = (pair[0:1] == expert) | (pair[1:2] == expert)
    named = jnp.broadcast_to(jnp.where(named, 1.0, 0.0), (capacity, token_count))
    rank = dot(named.astype(BF16), earlier)
    slot = lax.broadcasted_iota(jnp.int32, (capacity, token_count), 0).astype(F32)
    return jnp.where(rank == slot, named, 0.0).astype(BF16)


ROUTE_ROWS = 16


def cut_columns(rows, pair, group, targets, groups, block):
    def end_of(index):
        return jnp.where(index < groups // 2, 0, groups - 1)

    token_count, width = rows.shape
    lines = token_count + ROUTE_ROWS
    if block % 128:
        wide = -(-block // 128) * 128

        def tail(columns):
            return jnp.pad(pair.astype(BF16), ((0, ROUTE_ROWS - 2), (0, columns - token_count)))

        def cut(index):
            return jnp.concatenate([cut_padded(rows, [index], block, wide), tail(wide)], axis=0)

        return [jnp.concatenate([rows, tail(width)], axis=0)] + [
            jnp.concatenate([cut(t)] + ([cut(end_of(t))] if k else []), axis=1) for k, t in enumerate(targets)
        ]
    scalars = targets + [end_of(t) for t in targets[1:]]
    count = len(targets)

    def body(s, ins, outs):
        held = jnp.concatenate([ins[0][...].astype(F32), jnp.zeros((ROUTE_ROWS - 2, token_count), F32)], axis=0)
        for i, o in zip(ins[1:], outs):
            o[:token_count] = i[...]
            o[token_count:] = jnp.zeros((ROUTE_ROWS, block), BF16)
            o[token_count:, :token_count] = held.astype(BF16)

    def from_block(k):
        if k == 0:
            return lambda j, s: (0, s[0])
        return lambda j, s: (0, jnp.where(j == 0, s[k], s[count + k - 1]))

    return call(
        body,
        "cut_columns",
        scalars,
        [pair] + [rows] * (count + 1),
        [whole(pair.shape), pl.BlockSpec((token_count, block), lambda j, s: (0, j))]
        + [pl.BlockSpec((token_count, block), from_block(k)) for k in range(count)],
        [((lines, width), BF16)] + [((lines, block * (1 if k == 0 else 2)), BF16) for k in range(count)],
        [pl.BlockSpec((lines, block), lambda j, s: (0, j))]
        + [
            pl.BlockSpec(
                (lines, block), (lambda j, s: (0, 0)) if k == 0 else (lambda j, s: (0, jnp.minimum(j, 1)))
            )
            for k in range(count)
        ],
        (groups,),
    )


def cut_padded(rows, indices, block, wide):
    pieces = [lax.dynamic_slice_in_dim(rows, i * block, block, axis=1) for i in indices]
    return jnp.concatenate([jnp.pad(p, ((0, 0), (0, wide - block))) for p in pieces], axis=1)


def join_columns(pieces, after=()):
    lines = pieces[0][0].shape[0]
    total = sum(size for _, _, size in pieces)

    def body(s, ins, outs):
        at = 0
        for ref, (_, first, size) in zip(ins, pieces):
            outs[0][:, at : at + size] = ref[...]
            at += size

    return call(
        body,
        "join_columns",
        [jnp.int32(0)],
        [array for array, _, _ in pieces],
        [pl.BlockSpec((lines, size), lambda j, s, c=first // size: (0, c)) for _, first, size in pieces],
        [((lines, total), BF16)],
        [whole((lines, total))],
        (1,),
        after=after,
    )[0]


def forward(expert, places, rows, upstream, gate_w, up_w, up_parts, first=None, after=()):
    sources = len(rows)
    lines, width = rows[0].shape
    token_count = lines - ROUTE_ROWS
    slots, hidden = upstream.shape
    capacity = slots // len(places)
    skip = 0 if first is None else len(places) - sources
    used = places[skip : skip + sources]
    step = 256 if hidden % 256 == 0 else hidden
    count = sources * capacity
    lead = skip * capacity
    spans, at = [], 0
    for size in up_parts:
        spans.append((at // step, (at + size) // step))
        at += size

    def body(s, ins, refs):
        tok = ins[:sources]
        up_ref, wg, wu = ins[sources : sources + 3]
        gate_out, up_outs, received = refs[0], refs[1:-1], refs[-1]
        j = pl.program_id(0)

        @pl.when(pl.program_id(0) == 0)
        def _():
            earlier = earlier_mask(token_count)
            for r in range(sources):
                mark = slot_marks(pair_in(tok[r], token_count), s[0], capacity, earlier)
                received[r * capacity : (r + 1) * capacity] = dot(mark, tok[r][:token_count]).astype(BF16)

        gate = dot(received[...], wg[...])
        up = dot(received[...], wu[...])
        for r in range(sources):
            here = slice(r * capacity, (r + 1) * capacity)
            g = gate[here]
            h = up_ref[pl.ds(pl.multiple_of(s[1 + r] * capacity, 16), capacity), :].astype(F32)
            sig = jax.nn.sigmoid(g)
            gate_out[here] = (h * up[here] * sig * (1.0 + g * (1.0 - sig))).astype(BF16)
            up_grad = (h * g * sig).astype(BF16)
            for (low, high), out in zip(spans, up_outs):

                @pl.when((j >= low) & (j < high))
                def _():
                    out[lead + r * capacity : lead + (r + 1) * capacity] = up_grad

        if first is not None:
            for (low, high), out in zip(spans, up_outs):

                @pl.when((j >= low) & (j < high))
                def _():
                    out[:lead] = ins[sources + 3][...]

    ins = list(rows) + [upstream, gate_w, up_w]
    specs = [whole((lines, width))] * sources
    specs += [pl.BlockSpec((slots, step), lambda j, s: (0, j))]
    specs += [pl.BlockSpec((width, step), lambda j, s: (0, j))] * 2
    if first is not None:
        ins.append(first)
        specs.append(pl.BlockSpec((lead, step), lambda j, s: (0, j)))
    return call(
        body,
        "forward_first" if first is None else "forward_rest",
        [expert] + used,
        ins,
        specs,
        [((count, hidden), BF16)] + [((lead + count, size), BF16) for size in up_parts],
        [pl.BlockSpec((count, step), lambda j, s: (0, j))]
        + [
            pl.BlockSpec((lead + count, step), lambda j, s, a=low, b=high: (0, jnp.clip(j - a, 0, b - a - 1)))
            for low, high in spans
        ],
        (hidden // step,),
        scratch=[pltpu.VMEM((count, width), BF16)],
        after=after,
        vmem=60,
    )


def halves_of(width):
    step = 512 if width % 512 == 0 else 128
    steps = width // step
    return step, steps, (steps + 1) // 2


def slot_gradients(places, gate, ups, gate_w, up_w, near=None, after=()):
    width, hidden = gate_w.shape
    count = gate.shape[0]
    skip = 0 if near is None else near.shape[0]
    slots = skip + count
    capacity = slots // len(places) if skip else count // 2
    step, steps, lead = halves_of(width)

    def body(s, ins, outs):
        j = pl.program_id(0)
        wg, wu = ins[0], ins[1]
        across = ((1,), (1,))
        total = dot(ins[2][...], wg[...], across)
        at = 0
        for g in ins[3 : 3 + len(ups)]:
            size = g.shape[1]
            total = total + dot(g[skip:], wu[:, at : at + size], across)
            at += size
        total = total.astype(BF16)
        if near is None:
            outs[0][...] = total
            return

        def put(out):
            for r in range(len(places)):
                at = pl.ds(pl.multiple_of(s[r] * capacity, 16), capacity)
                if r < 2:
                    out[at, :] = ins[-1][r * capacity : (r + 1) * capacity]
                else:
                    out[at, :] = total[(r - 2) * capacity : (r - 1) * capacity]

        @pl.when(j < lead)
        def _():
            put(outs[0])

        @pl.when(j >= lead)
        def _():
            put(outs[1])

    ins = [gate_w, up_w, gate] + list(ups)
    specs = [pl.BlockSpec((step, hidden), lambda j, s: (j, 0))] * 2 + [whole(g.shape) for g in ins[2:]]
    if near is None:
        outs = [((slots, width), BF16)]
        out_specs = [pl.BlockSpec((slots, step), lambda j, s: (0, j))]
    else:
        ins.append(near)
        specs.append(pl.BlockSpec((skip, step), lambda j, s: (0, j)))
        outs = [((slots, lead * step), BF16), ((slots, width - lead * step), BF16)]
        out_specs = [
            pl.BlockSpec((slots, step), lambda j, s: (0, jnp.minimum(j, lead - 1))),
            pl.BlockSpec((slots, step), lambda j, s: (0, jnp.maximum(j - lead, 0))),
        ]
    out = call(
        body,
        "near_gradients" if near is None else "slot_gradients",
        places,
        ins,
        specs,
        outs,
        out_specs,
        (steps,),
        after=after,
        vmem=60,
    )
    return out[0] if near is None else out


def combine(pair, returned, experts, after=()):
    token_count = pair.shape[1]
    slots, width = returned.shape
    capacity = slots // experts
    step = 512 if width % 512 == 0 else 128

    def body(s, ins, refs):
        marks = refs[-1]

        @pl.when(pl.program_id(0) == 0)
        def _():
            earlier = earlier_mask(token_count)
            for r in range(experts):
                marks[r * capacity : (r + 1) * capacity] = slot_marks(ins[0][...], r, capacity, earlier)

        refs[0][...] = dot(marks[...], ins[1][...], ((0,), (0,))).astype(BF16)

    return call(
        body,
        "combine",
        [jnp.int32(0)],
        [pair, returned],
        [whole(pair.shape), pl.BlockSpec((slots, step), lambda j, s: (0, j))],
        [((token_count, width), BF16)],
        [pl.BlockSpec((token_count, step), lambda j, s: (0, j))],
        (width // step,),
        scratch=[pltpu.VMEM((slots, token_count), BF16)],
        after=after,
    )[0]


def pick_rows(expert, blocks, rows, capacity, block, routes=None, after=()):
    sources = len(rows)
    lines = rows[0].shape[0]
    token_count = lines - ROUTE_ROWS
    count = len(blocks)

    def body(s, ins, outs):
        earlier = earlier_mask(token_count)
        picked = []
        for r in range(sources):
            pair = pair_in(ins[r], token_count) if routes is None else ins[sources + r][...]
            pair = pair.astype(F32).astype(jnp.int32)
            mark = slot_marks(pair, s[0], capacity, earlier)
            picked.append(dot(mark, ins[r][:token_count]))
        outs[0][...] = jnp.concatenate(picked, axis=0).astype(BF16).T

    ins, specs = list(rows), []
    for r in range(sources):
        specs.append(pl.BlockSpec((lines, block), lambda j, s: (0, s[1 + j])))
    if routes is not None:
        ins += list(routes)
        specs += [
            pl.BlockSpec((ROUTE_ROWS, token_count), lambda j, s: (token_count // ROUTE_ROWS, 0)) for _ in routes
        ]
    return call(
        body,
        "pick_rows",
        [expert] + list(blocks),
        ins,
        specs,
        [((count * block, sources * capacity), BF16)],
        [pl.BlockSpec((block, sources * capacity), lambda j, s: (j, 0))],
        (count,),
        after=after,
    )[0]


def products(terms, block, part, dtype, name, extras=(), total=None, after=(), vmem=28):
    slots = terms[0][0].shape[1]
    split = 2 if block % 32 == 0 else 1
    lines = block // split

    count = len(terms)
    pieces = sum(len(parts) for _, _, parts in terms)

    def body(s, ins, outs):
        left = jnp.concatenate([p[...] for p in ins[:count]], axis=1)
        right = jnp.concatenate([g[...] for g in ins[count : count + pieces]], axis=0)
        result = dot(left, right)
        if extras:
            result = result + jnp.concatenate([e[...].astype(F32) for e in ins[count + pieces :]], axis=1)
        outs[0][...] = result.astype(dtype)

    ins = [p for p, _, _ in terms]
    specs = [pl.BlockSpec((lines, slots), lambda j, s, i=i: (i * split + j, 0)) for _, i, _ in terms]
    for _, _, parts in terms:
        for array, column in parts:
            ins.append(array)
            specs.append(pl.BlockSpec((array.shape[0], part), lambda j, s, c=column: (0, c)))
    for e in extras:
        ins.append(e)
        specs.append(pl.BlockSpec((lines, e.shape[1]), lambda j, s: (j, 0)))
    return call(
        body,
        name,
        [jnp.int32(0)],
        ins,
        specs,
        [((block, total or part), dtype)],
        [pl.BlockSpec((lines, part), lambda j, s: (j, 0))],
        (split,),
        after=after,
        vmem=vmem,
    )[0]


def finish(own, extra, target, place, total, after=()):
    block, part = own.shape
    ins = [own, extra]
    specs = [whole((block, part))] * 2
    if target is not None:
        ins.append(target)
        specs.append(pl.BlockSpec(memory_space=pl.ANY))

    def body(s, refs, outs):
        outs[0][...] = (refs[0][...] + refs[1][...].astype(F32)).astype(BF16)

    return call(
        body,
        "finish",
        [jnp.int32(0)],
        ins,
        specs,
        [((block, total), BF16)],
        [pl.BlockSpec((block, part), lambda j, s: (0, place))],
        (1,),
        after=after,
        aliases={3: 0} if target is not None else None,
        vmem=60,
    )[0]


def tied(value, *others):
    return lax.optimization_barrier((value,) + others)[0]


def shards(tokens, routes, hidden_grad, w_gate, w_up):
    groups = lax.axis_size("dp")
    experts = lax.axis_size("expert")
    sections = lax.axis_size("section")
    group = lax.axis_index("dp")
    expert = lax.axis_index("expert")
    rows = tokens[0]
    token_count, width = rows.shape
    slots = hidden_grad.shape[3]
    capacity = slots // experts
    hidden = w_gate.shape[3]
    block = width // groups
    gate_w = w_gate[0, 0]
    up_w = w_up[0, 0]
    upstream = hidden_grad[0, 0, 0]
    sets = grouped_pairs(groups)
    up_parts = [hidden // 2, hidden // 2]
    wide = -(-block // 128) * 128
    own_blocks = [group, jnp.where(group < groups // 2, 0, groups - 1)]

    def swap(value):
        return lax.ppermute(value, "expert", [(s, s ^ 1) for s in range(experts)])

    def shift(value, by):
        return lax.ppermute(value, "expert", [(s, (s + 2 * by) % experts) for s in range(experts)])

    def over_groups(value, pairs):
        return lax.ppermute(value, "dp", pairs)

    def to_sources(value):
        back = lax.all_to_all(
            value.reshape(experts, capacity, value.shape[1]), "expert", split_axis=0, concat_axis=0, tiled=True
        )
        return back.reshape(value.shape)

    def passed_on(value):
        return lax.ppermute(value, "section", [(s, (s - 1) % sections) for s in range(sections)])

    def to_ends(value):
        return lax.ppermute(value, "dp", [(1, 0), (groups - 2, groups - 1)])

    chips = range(1, experts // 2)
    places = [jnp.bitwise_xor((expert - 2 * (r // 2)) % experts, r % 2) for r in range(experts)]
    targets = [target_in(pairs, group) for pairs in sets]
    order = list(range(2, len(sets))) + [1, 0]

    pair = routes[0].T
    own, *cut = cut_columns(rows, pair, group, targets, groups, block)
    far_even = [shift(own, by) for by in chips]
    others = {k: over_groups(cut[k], sets[k]) for k in order}
    partner = swap(own)
    near_gate, near_up = forward(expert, places, [own, partner], upstream, gate_w, up_w, [hidden])
    near_back = slot_gradients(places, near_gate, [near_up], gate_w, up_w, after=[near_gate])
    epoch = [others[k] for k in order] + far_even + [near_back]

    near_sent = {k: over_groups(tied(near_gate, *epoch), sets[k]) for k in order}
    far = []
    for value in far_even:
        far += [value, swap(tied(value, *epoch))]
    end_columns = join_columns([(others[k], wide, wide) for k in range(1, len(sets))], after=epoch[:-1])
    end_far = [shift(end_columns, by) for by in chips]
    far_gate, *ups = forward(
        expert, places, far, upstream, gate_w, up_w, up_parts, first=near_up, after=[end_columns]
    )
    own_columns = [own, partner] + far
    own_lines = own_columns
    if wide != block:
        own_columns = [cut_padded(v, own_blocks, block, wide) for v in own_columns]
        own_blocks = [jnp.int32(0), jnp.int32(1)]
    own_picked = pick_rows(
        expert, own_blocks, own_columns, capacity, wide, routes=own_lines, after=[far_gate]
    )
    own_part = join_columns([(others[k], 0, wide) for k in range(len(sets))], after=[own_picked])
    epoch = [near_sent[k] for k in order] + [own_part]

    far_sent = {k: over_groups(tied(far_gate, *epoch), sets[k]) for k in order}
    first_back, second_back = slot_gradients(
        places, far_gate, ups, gate_w, up_w, near=near_back, after=epoch
    )
    first_back = to_sources(first_back)
    end_rows = []
    for value in [end_columns] + end_far:
        end_rows += [value, swap(tied(value, *epoch))]
    column_far = [shift(tied(own_part, *epoch), by) for by in chips]
    end_picked = pick_rows(
        expert, [jnp.int32(k) for k in range(len(sets) - 1)], end_rows, capacity, wide, after=[second_back]
    )
    epoch = [far_sent[k] for k in order] + [end_picked]

    def parts_of(c):
        if c == 0:
            out = [[(near_gate, c), (far_gate, c)]]
            out += [[(near_sent[k], c), (far_sent[k], c)] for k in range(len(sets))]
        else:
            out = [[(ups[c - 1], 0)]] + [[(up_sent[c - 1][k], 0)] for k in range(len(sets))]
        return out

    def for_end(c, after):
        parts = parts_of(c)
        part = up_parts[c - 1] if c else hidden
        terms = [(own_picked, 1, parts[0])]
        terms += [(end_picked, k - 1, parts[1 + k]) for k in reversed(range(1, len(sets)))]
        return products(terms, wide, part, BF16, "for_end", after=after, vmem=60)

    def for_own(c, part, dtype, after, extras=(), total=None):
        parts = parts_of(c)
        terms = [(own_picked, 0, parts[0])]
        terms += [(picked, k, parts[1 + k]) for k in reversed(range(len(sets)))]
        return products(terms, wide, part, dtype, "for_own", extras=extras, total=total, after=after, vmem=60)

    up_sent = []

    def send_up(c):
        up_sent.append({k: over_groups(tied(ups[c], *epoch), sets[k]) for k in order})
        return [up_sent[c][k] for k in order]

    arriving = send_up(0)
    column_rows = []
    for value in [own_part] + column_far:
        column_rows += [value, swap(tied(value, *epoch))]
    end0 = for_end(0, epoch)
    extra0 = to_ends(end0)
    picked = pick_rows(
        expert, [jnp.int32(k) for k in range(len(sets))], column_rows, capacity, wide, after=[end0]
    )
    epoch = arriving + [picked, first_back]

    arriving = send_up(1)
    second_back = to_sources(tied(second_back, *epoch))
    end1 = for_end(1, epoch)
    extra1 = to_ends(end1)
    first_tok = combine(pair, first_back, experts, after=[end1])
    first_passed = passed_on(first_tok)
    gate = for_own(0, hidden, BF16, [first_tok], extras=[extra0])
    epoch = arriving + [gate]

    end2 = for_end(2, epoch)
    extra2 = to_ends(end2)
    second_tok = combine(pair, second_back, experts, after=[end2])
    second_passed = passed_on(second_tok)
    up0 = for_own(1, up_parts[0], BF16, [second_tok], extras=[extra1], total=hidden)
    own2 = for_own(2, up_parts[1], F32, [up0])
    passed = jnp.concatenate([tied(first_passed, own2), second_passed], axis=1)
    up1 = finish(own2, extra2, up0, up_parts[0] // up_parts[1], hidden)
    return (passed[None], gate[None, None, :block], up1[None, None, :block])


def solution(mesh):
    placed = (
        P("section", ("dp", "expert"), None),
        P("section", ("dp", "expert"), None),
        P("section", "dp", "expert", None, None),
        P("section", "expert", None, None),
        P("section", "expert", None, None),
    )
    return jax.shard_map(
        shards,
        mesh=mesh,
        in_specs=placed,
        out_specs=(
            P("section", ("dp", "expert"), None),
            P("section", "expert", "dp", None),
            P("section", "expert", "dp", None),
        ),
        check_vma=False,
    )
```

```python
import jax
import jax.numpy as jnp
from jax import lax
from jax.experimental import pallas as pl
from jax.experimental.pallas import tpu as pltpu
from jax.sharding import PartitionSpec as P

BF16 = jnp.bfloat16
F32 = jnp.float32
MIB = 1024 * 1024


def dot(a, b, contract=((1,), (0,))):
    return lax.dot_general(a, b, (contract, ((), ())), preferred_element_type=F32)


def grouped_pairs(count):
    first, last = 0, count - 1
    sets = []
    inner = range(1, last)
    for j, i in sorted(((j, i) for j in inner for i in inner if j != i), key=lambda p: (abs(p[0] - p[1]), p)):
        for chosen in sets:
            if all(j != a and i != b for a, b in chosen):
                chosen.append((j, i))
                break
        else:
            sets.append([(j, i)])
    out = [[(first, 1), (last, last - 1)]]
    for chosen in sets:
        out.append(chosen)
        out.append([({1: first, last - 1: last}[j], i) for j, i in chosen if j in (1, last - 1)])
    return out


def target_in(pairs, index):
    found = jnp.int32(0)
    for source, target in pairs:
        found = jnp.where(index == source, target, found)
    return found


def call(body, name, scalars, ins, in_specs, outs, out_specs, grid, scratch=(), after=(), aliases=None, vmem=28):
    count, skip = len(ins), len(after)

    def kernel(scalar_ref, *refs):
        body(scalar_ref, refs[:count], refs[count + skip :])

    return pl.pallas_call(
        kernel,
        name=name,
        out_shape=[jax.ShapeDtypeStruct(shape, dtype) for shape, dtype in outs],
        grid_spec=pltpu.PrefetchScalarGridSpec(
            num_scalar_prefetch=1,
            grid=grid,
            in_specs=list(in_specs) + [pl.BlockSpec(memory_space=pl.ANY)] * skip,
            out_specs=list(out_specs),
            scratch_shapes=list(scratch),
        ),
        input_output_aliases=aliases or {},
        compiler_params=pltpu.CompilerParams(
            dimension_semantics=("arbitrary",) * len(grid), vmem_limit_bytes=vmem * MIB
        ),
        cost_estimate=pl.CostEstimate(flops=1, bytes_accessed=1, transcendentals=0),
    )(jnp.stack(scalars).astype(jnp.int32), *ins, *after)


def whole(shape):
    return pl.BlockSpec(shape, lambda j, s: (0,) * len(shape))


def earlier_mask(token_count):
    first = lax.broadcasted_iota(jnp.int32, (token_count, token_count), 0)
    second = lax.broadcasted_iota(jnp.int32, (token_count, token_count), 1)
    return jnp.where(first < second, 1.0, 0.0).astype(BF16)


def pair_in(ref, token_count):
    return ref[token_count:, :token_count].astype(F32).astype(jnp.int32)


def slot_marks(pair, expert, capacity, earlier):
    token_count = pair.shape[1]
    named = (pair[0:1] == expert) | (pair[1:2] == expert)
    named = jnp.broadcast_to(jnp.where(named, 1.0, 0.0), (capacity, token_count))
    rank = dot(named.astype(BF16), earlier)
    slot = lax.broadcasted_iota(jnp.int32, (capacity, token_count), 0).astype(F32)
    return jnp.where(rank == slot, named, 0.0).astype(BF16)


ROUTE_ROWS = 16


def cut_columns(rows, pair, group, targets, groups, block):
    def end_of(index):
        return jnp.where(index < groups // 2, 0, groups - 1)

    token_count, width = rows.shape
    lines = token_count + ROUTE_ROWS
    if block % 128:
        wide = -(-block // 128) * 128

        def tail(columns):
            return jnp.pad(pair.astype(BF16), ((0, ROUTE_ROWS - 2), (0, columns - token_count)))

        def cut(index):
            return jnp.concatenate([cut_padded(rows, [index], block, wide), tail(wide)], axis=0)

        return [jnp.concatenate([rows, tail(width)], axis=0)] + [
            jnp.concatenate([cut(t)] + ([cut(end_of(t))] if k else []), axis=1) for k, t in enumerate(targets)
        ]
    scalars = targets + [end_of(t) for t in targets[1:]]
    count = len(targets)

    def body(s, ins, outs):
        held = jnp.concatenate([ins[0][...].astype(F32), jnp.zeros((ROUTE_ROWS - 2, token_count), F32)], axis=0)
        for i, o in zip(ins[1:], outs):
            o[:token_count] = i[...]
            o[token_count:] = jnp.zeros((ROUTE_ROWS, o.shape[1]), BF16)
            o[token_count:, :token_count] = held.astype(BF16)

    def from_block(k):
        if k == 0:
            return lambda j, s: (0, s[0])
        return lambda j, s: (0, jnp.where(j == 0, s[k], s[count + k - 1]))

    return call(
        body,
        "cut_columns",
        scalars,
        [pair] + [rows] * (count + 1),
        [whole(pair.shape), pl.BlockSpec((token_count, width // 2), lambda j, s: (0, j))]
        + [pl.BlockSpec((token_count, block), from_block(k)) for k in range(count)],
        [((lines, width), BF16)] + [((lines, block * (1 if k == 0 else 2)), BF16) for k in range(count)],
        [pl.BlockSpec((lines, width // 2), lambda j, s: (0, j))]
        + [
            pl.BlockSpec((lines, block), (lambda j, s: (0, 0)) if k == 0 else (lambda j, s: (0, j)))
            for k in range(count)
        ],
        (2,),
    )


def cut_padded(rows, indices, block, wide):
    pieces = [lax.dynamic_slice_in_dim(rows, i * block, block, axis=1) for i in indices]
    return jnp.concatenate([jnp.pad(p, ((0, 0), (0, wide - block))) for p in pieces], axis=1)


def join_columns(pieces, after=()):
    lines = pieces[0][0].shape[0]
    total = sum(size for _, _, size in pieces)

    def body(s, ins, outs):
        at = 0
        for ref, (_, first, size) in zip(ins, pieces):
            outs[0][:, at : at + size] = ref[...]
            at += size

    return call(
        body,
        "join_columns",
        [jnp.int32(0)],
        [array for array, _, _ in pieces],
        [pl.BlockSpec((lines, size), lambda j, s, c=first // size: (0, c)) for _, first, size in pieces],
        [((lines, total), BF16)],
        [whole((lines, total))],
        (1,),
        after=after,
    )[0]


def forward(expert, places, rows, upstream, gate_w, up_w, up_parts, first=None, after=()):
    sources = len(rows)
    lines, width = rows[0].shape
    token_count = lines - ROUTE_ROWS
    slots, hidden = upstream.shape
    capacity = slots // len(places)
    skip = 0 if first is None else len(places) - sources
    used = places[skip : skip + sources]
    step = 256 if hidden % 256 == 0 else hidden
    count = sources * capacity
    lead = skip * capacity
    spans, at = [], 0
    for size in up_parts:
        spans.append((at // step, (at + size) // step))
        at += size

    def body(s, ins, refs):
        tok = ins[:sources]
        up_ref, wg, wu = ins[sources : sources + 3]
        gate_out, up_outs, received = refs[0], refs[1:-1], refs[-1]
        j = pl.program_id(0)

        @pl.when(pl.program_id(0) == 0)
        def _():
            earlier = earlier_mask(token_count)
            for r in range(sources):
                mark = slot_marks(pair_in(tok[r], token_count), s[0], capacity, earlier)
                received[r * capacity : (r + 1) * capacity] = dot(mark, tok[r][:token_count]).astype(BF16)

        gate = dot(received[...], wg[...])
        up = dot(received[...], wu[...])
        for r in range(sources):
            here = slice(r * capacity, (r + 1) * capacity)
            g = gate[here]
            h = up_ref[pl.ds(pl.multiple_of(s[1 + r] * capacity, 16), capacity), :].astype(F32)
            sig = jax.nn.sigmoid(g)
            gate_out[here] = (h * up[here] * sig * (1.0 + g * (1.0 - sig))).astype(BF16)
            up_grad = (h * g * sig).astype(BF16)
            for (low, high), out in zip(spans, up_outs):

                @pl.when((j >= low) & (j < high))
                def _():
                    out[lead + r * capacity : lead + (r + 1) * capacity] = up_grad

        if first is not None:
            for (low, high), out in zip(spans, up_outs):

                @pl.when((j >= low) & (j < high))
                def _():
                    out[:lead] = ins[sources + 3][...]

    ins = list(rows) + [upstream, gate_w, up_w]
    specs = [whole((lines, width))] * sources
    specs += [pl.BlockSpec((slots, step), lambda j, s: (0, j))]
    specs += [pl.BlockSpec((width, step), lambda j, s: (0, j))] * 2
    if first is not None:
        ins.append(first)
        specs.append(pl.BlockSpec((lead, step), lambda j, s: (0, j)))
    return call(
        body,
        "forward_first" if first is None else "forward_rest",
        [expert] + used,
        ins,
        specs,
        [((count, hidden), BF16)] + [((lead + count, size), BF16) for size in up_parts],
        [pl.BlockSpec((count, step), lambda j, s: (0, j))]
        + [
            pl.BlockSpec((lead + count, step), lambda j, s, a=low, b=high: (0, jnp.clip(j - a, 0, b - a - 1)))
            for low, high in spans
        ],
        (hidden // step,),
        scratch=[pltpu.VMEM((count, width), BF16)],
        after=after,
        vmem=60,
    )


def halves_of(width):
    step = 512 if width % 512 == 0 else 128
    steps = width // step
    return step, steps, (steps + 1) // 2


def slot_gradients(places, gate, ups, gate_w, up_w, near=None, after=()):
    width, hidden = gate_w.shape
    count = gate.shape[0]
    skip = 0 if near is None else near.shape[0]
    slots = skip + count
    capacity = slots // len(places) if skip else count // 2
    step, steps, lead = halves_of(width)

    def body(s, ins, outs):
        j = pl.program_id(0)
        wg, wu = ins[0], ins[1]
        across = ((1,), (1,))
        total = dot(ins[2][...], wg[...], across)
        at = 0
        for g in ins[3 : 3 + len(ups)]:
            size = g.shape[1]
            total = total + dot(g[skip:], wu[:, at : at + size], across)
            at += size
        total = total.astype(BF16)
        if near is None:
            outs[0][...] = total
            return

        def put(out):
            for r in range(len(places)):
                at = pl.ds(pl.multiple_of(s[r] * capacity, 16), capacity)
                if r < 2:
                    out[at, :] = ins[-1][r * capacity : (r + 1) * capacity]
                else:
                    out[at, :] = total[(r - 2) * capacity : (r - 1) * capacity]

        @pl.when(j < lead)
        def _():
            put(outs[0])

        @pl.when(j >= lead)
        def _():
            put(outs[1])

    ins = [gate_w, up_w, gate] + list(ups)
    specs = [pl.BlockSpec((step, hidden), lambda j, s: (j, 0))] * 2 + [whole(g.shape) for g in ins[2:]]
    if near is None:
        outs = [((slots, width), BF16)]
        out_specs = [pl.BlockSpec((slots, step), lambda j, s: (0, j))]
    else:
        ins.append(near)
        specs.append(pl.BlockSpec((skip, step), lambda j, s: (0, j)))
        outs = [((slots, lead * step), BF16), ((slots, width - lead * step), BF16)]
        out_specs = [
            pl.BlockSpec((slots, step), lambda j, s: (0, jnp.minimum(j, lead - 1))),
            pl.BlockSpec((slots, step), lambda j, s: (0, jnp.maximum(j - lead, 0))),
        ]
    out = call(
        body,
        "near_gradients" if near is None else "slot_gradients",
        places,
        ins,
        specs,
        outs,
        out_specs,
        (steps,),
        after=after,
        vmem=60,
    )
    return out[0] if near is None else out


def combine(pair, returned, experts, after=()):
    token_count = pair.shape[1]
    slots, width = returned.shape
    capacity = slots // experts
    step = 512 if width % 512 == 0 else 128

    def body(s, ins, refs):
        marks = refs[-1]

        @pl.when(pl.program_id(0) == 0)
        def _():
            earlier = earlier_mask(token_count)
            for r in range(experts):
                marks[r * capacity : (r + 1) * capacity] = slot_marks(ins[0][...], r, capacity, earlier)

        refs[0][...] = dot(marks[...], ins[1][...], ((0,), (0,))).astype(BF16)

    return call(
        body,
        "combine",
        [jnp.int32(0)],
        [pair, returned],
        [whole(pair.shape), pl.BlockSpec((slots, step), lambda j, s: (0, j))],
        [((token_count, width), BF16)],
        [pl.BlockSpec((token_count, step), lambda j, s: (0, j))],
        (width // step,),
        scratch=[pltpu.VMEM((slots, token_count), BF16)],
        after=after,
    )[0]


def pick_rows(expert, blocks, rows, capacity, block, routes=None, after=()):
    sources = len(rows)
    lines = rows[0].shape[0]
    token_count = lines - ROUTE_ROWS
    count = len(blocks)

    def body(s, ins, outs):
        earlier = earlier_mask(token_count)
        picked = []
        for r in range(sources):
            pair = pair_in(ins[r], token_count) if routes is None else ins[sources + r][...]
            pair = pair.astype(F32).astype(jnp.int32)
            mark = slot_marks(pair, s[0], capacity, earlier)
            picked.append(dot(mark, ins[r][:token_count]))
        outs[0][...] = jnp.concatenate(picked, axis=0).astype(BF16).T

    ins, specs = list(rows), []
    for r in range(sources):
        specs.append(pl.BlockSpec((lines, block), lambda j, s: (0, s[1 + j])))
    if routes is not None:
        ins += list(routes)
        specs += [
            pl.BlockSpec((ROUTE_ROWS, token_count), lambda j, s: (token_count // ROUTE_ROWS, 0)) for _ in routes
        ]
    return call(
        body,
        "pick_rows",
        [expert] + list(blocks),
        ins,
        specs,
        [((count * block, sources * capacity), BF16)],
        [pl.BlockSpec((block, sources * capacity), lambda j, s: (j, 0))],
        (count,),
        after=after,
    )[0]


def products(terms, block, part, dtype, name, extras=(), total=None, after=(), vmem=28):
    slots = terms[0][0].shape[1]
    split = 2 if block % 32 == 0 else 1
    lines = block // split

    count = len(terms)
    pieces = sum(len(parts) for _, _, parts in terms)

    def body(s, ins, outs):
        left = jnp.concatenate([p[...] for p in ins[:count]], axis=1)
        right = jnp.concatenate([g[...] for g in ins[count : count + pieces]], axis=0)
        result = dot(left, right)
        if extras:
            result = result + jnp.concatenate([e[...].astype(F32) for e in ins[count + pieces :]], axis=1)
        outs[0][...] = result.astype(dtype)

    ins = [p for p, _, _ in terms]
    specs = [pl.BlockSpec((lines, slots), lambda j, s, i=i: (i * split + j, 0)) for _, i, _ in terms]
    for _, _, parts in terms:
        for array, column in parts:
            ins.append(array)
            specs.append(pl.BlockSpec((array.shape[0], part), lambda j, s, c=column: (0, c)))
    for e in extras:
        ins.append(e)
        specs.append(pl.BlockSpec((lines, e.shape[1]), lambda j, s: (j, 0)))
    return call(
        body,
        name,
        [jnp.int32(0)],
        ins,
        specs,
        [((block, total or part), dtype)],
        [pl.BlockSpec((lines, part), lambda j, s: (j, 0))],
        (split,),
        after=after,
        vmem=vmem,
    )[0]


def finish(own, extra, target, place, total, after=()):
    block, part = own.shape
    ins = [own, extra]
    specs = [whole((block, part))] * 2
    if target is not None:
        ins.append(target)
        specs.append(pl.BlockSpec(memory_space=pl.ANY))

    def body(s, refs, outs):
        outs[0][...] = (refs[0][...] + refs[1][...].astype(F32)).astype(BF16)

    return call(
        body,
        "finish",
        [jnp.int32(0)],
        ins,
        specs,
        [((block, total), BF16)],
        [pl.BlockSpec((block, part), lambda j, s: (0, place))],
        (1,),
        after=after,
        aliases={3: 0} if target is not None else None,
        vmem=60,
    )[0]


def tied(value, *others):
    return lax.optimization_barrier((value,) + others)[0]


def shards(tokens, routes, hidden_grad, w_gate, w_up):
    groups = lax.axis_size("dp")
    experts = lax.axis_size("expert")
    sections = lax.axis_size("section")
    group = lax.axis_index("dp")
    expert = lax.axis_index("expert")
    rows = tokens[0]
    token_count, width = rows.shape
    slots = hidden_grad.shape[3]
    capacity = slots // experts
    hidden = w_gate.shape[3]
    block = width // groups
    gate_w = w_gate[0, 0]
    up_w = w_up[0, 0]
    upstream = hidden_grad[0, 0, 0]
    sets = grouped_pairs(groups)
    up_parts = [hidden // 2, hidden // 2]
    wide = -(-block // 128) * 128
    own_blocks = [group, jnp.where(group < groups // 2, 0, groups - 1)]

    def swap(value):
        return lax.ppermute(value, "expert", [(s, s ^ 1) for s in range(experts)])

    def shift(value, by):
        return lax.ppermute(value, "expert", [(s, (s + 2 * by) % experts) for s in range(experts)])

    def over_groups(value, pairs):
        return lax.ppermute(value, "dp", pairs)

    def to_sources(value):
        back = lax.all_to_all(
            value.reshape(experts, capacity, value.shape[1]), "expert", split_axis=0, concat_axis=0, tiled=True
        )
        return back.reshape(value.shape)

    def passed_on(value):
        return lax.ppermute(value, "section", [(s, (s - 1) % sections) for s in range(sections)])

    def to_ends(value):
        return lax.ppermute(value, "dp", [(1, 0), (groups - 2, groups - 1)])

    chips = range(1, experts // 2)
    places = [jnp.bitwise_xor((expert - 2 * (r // 2)) % experts, r % 2) for r in range(experts)]
    targets = [target_in(pairs, group) for pairs in sets]
    order = list(range(2, len(sets))) + [1, 0]

    pair = routes[0].T
    own, *cut = cut_columns(rows, pair, group, targets, groups, block)
    far_even = [shift(own, by) for by in chips]
    others = {k: over_groups(cut[k], sets[k]) for k in order}
    partner = swap(own)
    near_gate, near_up = forward(expert, places, [own, partner], upstream, gate_w, up_w, [hidden])
    near_back = slot_gradients(places, near_gate, [near_up], gate_w, up_w, after=[near_gate])
    epoch = [others[k] for k in order] + far_even + [near_back]

    near_sent = {k: over_groups(tied(near_gate, *epoch), sets[k]) for k in order}
    far = []
    for value in far_even:
        far += [value, swap(tied(value, *epoch))]
    end_columns = join_columns([(others[k], wide, wide) for k in range(1, len(sets))], after=epoch[:-1])
    end_far = [shift(end_columns, by) for by in chips]
    far_gate, *ups = forward(
        expert, places, far, upstream, gate_w, up_w, up_parts, first=near_up, after=[end_columns]
    )
    own_columns = [own, partner] + far
    own_lines = own_columns
    if wide != block:
        own_columns = [cut_padded(v, own_blocks, block, wide) for v in own_columns]
        own_blocks = [jnp.int32(0), jnp.int32(1)]
    own_picked = pick_rows(
        expert, own_blocks, own_columns, capacity, wide, routes=own_lines, after=[far_gate]
    )
    own_part = join_columns([(others[k], 0, wide) for k in range(len(sets))], after=[own_picked])
    epoch = [near_sent[k] for k in order] + [own_part]

    far_sent = {k: over_groups(tied(far_gate, *epoch), sets[k]) for k in order}
    first_back, second_back = slot_gradients(
        places, far_gate, ups, gate_w, up_w, near=near_back, after=epoch
    )
    first_back = to_sources(first_back)
    end_rows = []
    for value in [end_columns] + end_far:
        end_rows += [value, swap(tied(value, *epoch))]
    column_far = [shift(tied(own_part, *epoch), by) for by in chips]
    end_picked = pick_rows(
        expert, [jnp.int32(k) for k in range(len(sets) - 1)], end_rows, capacity, wide, after=[second_back]
    )
    epoch = [far_sent[k] for k in order] + [end_picked]

    def parts_of(c):
        if c == 0:
            out = [[(near_gate, c), (far_gate, c)]]
            out += [[(near_sent[k], c), (far_sent[k], c)] for k in range(len(sets))]
        else:
            out = [[(ups[c - 1], 0)]] + [[(up_sent[c - 1][k], 0)] for k in range(len(sets))]
        return out

    def for_end(c, after):
        parts = parts_of(c)
        part = up_parts[c - 1] if c else hidden
        terms = [(own_picked, 1, parts[0])]
        terms += [(end_picked, k - 1, parts[1 + k]) for k in reversed(range(1, len(sets)))]
        return products(terms, wide, part, BF16, "for_end", after=after, vmem=60)

    def for_own(c, part, dtype, after, extras=(), total=None):
        parts = parts_of(c)
        terms = [(own_picked, 0, parts[0])]
        terms += [(picked, k, parts[1 + k]) for k in reversed(range(len(sets)))]
        return products(terms, wide, part, dtype, "for_own", extras=extras, total=total, after=after, vmem=60)

    up_sent = []

    def send_up(c):
        up_sent.append({k: over_groups(tied(ups[c], *epoch), sets[k]) for k in order})
        return [up_sent[c][k] for k in order]

    arriving = send_up(0)
    column_rows = []
    for value in [own_part] + column_far:
        column_rows += [value, swap(tied(value, *epoch))]
    end0 = for_end(0, epoch)
    extra0 = to_ends(end0)
    picked = pick_rows(
        expert, [jnp.int32(k) for k in range(len(sets))], column_rows, capacity, wide, after=[end0]
    )
    epoch = arriving + [picked, first_back]

    arriving = send_up(1)
    second_back = to_sources(tied(second_back, *epoch))
    end1 = for_end(1, epoch)
    extra1 = to_ends(end1)
    first_tok = combine(pair, first_back, experts, after=[end1])
    first_passed = passed_on(first_tok)
    gate = for_own(0, hidden, BF16, [first_tok], extras=[extra0])
    epoch = arriving + [gate]

    end2 = for_end(2, epoch)
    extra2 = to_ends(end2)
    second_tok = combine(pair, second_back, experts, after=[end2])
    second_passed = passed_on(second_tok)
    up0 = for_own(1, up_parts[0], BF16, [second_tok], extras=[extra1], total=hidden)
    own2 = for_own(2, up_parts[1], F32, [up0])
    passed = jnp.concatenate([tied(first_passed, own2), second_passed], axis=1)
    up1 = finish(own2, extra2, up0, up_parts[0] // up_parts[1], hidden)
    return (passed[None], gate[None, None, :block], up1[None, None, :block])


def solution(mesh):
    placed = (
        P("section", ("dp", "expert"), None),
        P("section", ("dp", "expert"), None),
        P("section", "dp", "expert", None, None),
        P("section", "expert", None, None),
        P("section", "expert", None, None),
    )
    return jax.shard_map(
        shards,
        mesh=mesh,
        in_specs=placed,
        out_specs=(
            P("section", ("dp", "expert"), None),
            P("section", "expert", "dp", None),
            P("section", "expert", "dp", None),
        ),
        check_vma=False,
    )
```

```python
import jax
import jax.numpy as jnp
from jax import lax
from jax.experimental import pallas as pl
from jax.experimental.pallas import tpu as pltpu
from jax.sharding import PartitionSpec as P

BF16 = jnp.bfloat16
F32 = jnp.float32
MIB = 1024 * 1024


def dot(a, b, contract=((1,), (0,))):
    return lax.dot_general(a, b, (contract, ((), ())), preferred_element_type=F32)


def grouped_pairs(count):
    first, last = 0, count - 1
    sets = []
    inner = range(1, last)
    for j, i in sorted(((j, i) for j in inner for i in inner if j != i), key=lambda p: (abs(p[0] - p[1]), p)):
        for chosen in sets:
            if all(j != a and i != b for a, b in chosen):
                chosen.append((j, i))
                break
        else:
            sets.append([(j, i)])
    out = [[(first, 1), (last, last - 1)]]
    for chosen in sets:
        out.append(chosen)
        out.append([({1: first, last - 1: last}[j], i) for j, i in chosen if j in (1, last - 1)])
    return out


def target_in(pairs, index):
    found = jnp.int32(0)
    for source, target in pairs:
        found = jnp.where(index == source, target, found)
    return found


def call(body, name, scalars, ins, in_specs, outs, out_specs, grid, scratch=(), after=(), aliases=None, vmem=28):
    count, skip = len(ins), len(after)

    def kernel(scalar_ref, *refs):
        body(scalar_ref, refs[:count], refs[count + skip :])

    return pl.pallas_call(
        kernel,
        name=name,
        out_shape=[jax.ShapeDtypeStruct(shape, dtype) for shape, dtype in outs],
        grid_spec=pltpu.PrefetchScalarGridSpec(
            num_scalar_prefetch=1,
            grid=grid,
            in_specs=list(in_specs) + [pl.BlockSpec(memory_space=pl.ANY)] * skip,
            out_specs=list(out_specs),
            scratch_shapes=list(scratch),
        ),
        input_output_aliases=aliases or {},
        compiler_params=pltpu.CompilerParams(
            dimension_semantics=("arbitrary",) * len(grid), vmem_limit_bytes=vmem * MIB
        ),
        cost_estimate=pl.CostEstimate(flops=1, bytes_accessed=1, transcendentals=0),
    )(jnp.stack(scalars).astype(jnp.int32), *ins, *after)


def whole(shape):
    return pl.BlockSpec(shape, lambda j, s: (0,) * len(shape))


def earlier_mask(token_count):
    first = lax.broadcasted_iota(jnp.int32, (token_count, token_count), 0)
    second = lax.broadcasted_iota(jnp.int32, (token_count, token_count), 1)
    return jnp.where(first < second, 1.0, 0.0).astype(BF16)


def pair_in(ref, token_count):
    return ref[token_count:, :token_count].astype(F32).astype(jnp.int32)


def slot_marks(pair, expert, capacity, earlier):
    token_count = pair.shape[1]
    named = (pair[0:1] == expert) | (pair[1:2] == expert)
    named = jnp.broadcast_to(jnp.where(named, 1.0, 0.0), (capacity, token_count))
    rank = dot(named.astype(BF16), earlier)
    slot = lax.broadcasted_iota(jnp.int32, (capacity, token_count), 0).astype(F32)
    return jnp.where(rank == slot, named, 0.0).astype(BF16)


ROUTE_ROWS = 16


def cut_columns(rows, pair, group, targets, groups, block):
    def end_of(index):
        return jnp.where(index < groups // 2, 0, groups - 1)

    token_count, width = rows.shape
    lines = token_count + ROUTE_ROWS
    if block % 128:
        wide = -(-block // 128) * 128

        def tail(columns):
            return jnp.pad(pair.astype(BF16), ((0, ROUTE_ROWS - 2), (0, columns - token_count)))

        def cut(index):
            return jnp.concatenate([cut_padded(rows, [index], block, wide), tail(wide)], axis=0)

        return [jnp.concatenate([rows, tail(width)], axis=0)] + [
            jnp.concatenate([cut(t)] + ([cut(end_of(t))] if k else []), axis=1) for k, t in enumerate(targets)
        ]
    scalars = targets + [end_of(t) for t in targets[1:]]
    count = len(targets)

    def body(s, ins, outs):
        held = jnp.concatenate([ins[0][...].astype(F32), jnp.zeros((ROUTE_ROWS - 2, token_count), F32)], axis=0)
        for i, o in zip(ins[1:], outs):
            o[:token_count] = i[...]
            o[token_count:] = jnp.zeros((ROUTE_ROWS, o.shape[1]), BF16)
            o[token_count:, :token_count] = held.astype(BF16)

    def from_block(k):
        if k == 0:
            return lambda j, s: (0, s[0])
        return lambda j, s: (0, jnp.where(j == 0, s[k], s[count + k - 1]))

    return call(
        body,
        "cut_columns",
        scalars,
        [pair] + [rows] * (count + 1),
        [whole(pair.shape), pl.BlockSpec((token_count, width // 2), lambda j, s: (0, j))]
        + [pl.BlockSpec((token_count, block), from_block(k)) for k in range(count)],
        [((lines, width), BF16)] + [((lines, block * (1 if k == 0 else 2)), BF16) for k in range(count)],
        [pl.BlockSpec((lines, width // 2), lambda j, s: (0, j))]
        + [
            pl.BlockSpec((lines, block), (lambda j, s: (0, 0)) if k == 0 else (lambda j, s: (0, j)))
            for k in range(count)
        ],
        (2,),
    )


def cut_padded(rows, indices, block, wide):
    pieces = [lax.dynamic_slice_in_dim(rows, i * block, block, axis=1) for i in indices]
    return jnp.concatenate([jnp.pad(p, ((0, 0), (0, wide - block))) for p in pieces], axis=1)


def join_columns(pieces, after=()):
    lines = pieces[0][0].shape[0]
    total = sum(size for _, _, size in pieces)

    def body(s, ins, outs):
        at = 0
        for ref, (_, first, size) in zip(ins, pieces):
            outs[0][:, at : at + size] = ref[...]
            at += size

    return call(
        body,
        "join_columns",
        [jnp.int32(0)],
        [array for array, _, _ in pieces],
        [pl.BlockSpec((lines, size), lambda j, s, c=first // size: (0, c)) for _, first, size in pieces],
        [((lines, total), BF16)],
        [whole((lines, total))],
        (1,),
        after=after,
    )[0]


def forward(expert, places, rows, upstream, gate_w, up_w, up_parts, first=None, after=()):
    sources = len(rows)
    lines, width = rows[0].shape
    token_count = lines - ROUTE_ROWS
    slots, hidden = upstream.shape
    capacity = slots // len(places)
    skip = 0 if first is None else len(places) - sources
    used = places[skip : skip + sources]
    step = 256 if hidden % 256 == 0 else hidden
    count = sources * capacity
    lead = skip * capacity
    spans, at = [], 0
    for size in up_parts:
        spans.append((at // step, (at + size) // step))
        at += size

    def body(s, ins, refs):
        tok = ins[:sources]
        up_ref, wg, wu = ins[sources : sources + 3]
        gate_out, up_outs, received = refs[0], refs[1:-1], refs[-1]
        j = pl.program_id(0)

        @pl.when(pl.program_id(0) == 0)
        def _():
            earlier = earlier_mask(token_count)
            for r in range(sources):
                mark = slot_marks(pair_in(tok[r], token_count), s[0], capacity, earlier)
                received[r * capacity : (r + 1) * capacity] = dot(mark, tok[r][:token_count]).astype(BF16)

        gate = dot(received[...], wg[...])
        up = dot(received[...], wu[...])
        for r in range(sources):
            here = slice(r * capacity, (r + 1) * capacity)
            g = gate[here]
            h = up_ref[pl.ds(pl.multiple_of(s[1 + r] * capacity, 16), capacity), :].astype(F32)
            sig = jax.nn.sigmoid(g)
            gate_out[here] = (h * up[here] * sig * (1.0 + g * (1.0 - sig))).astype(BF16)
            up_grad = (h * g * sig).astype(BF16)
            for (low, high), out in zip(spans, up_outs):

                @pl.when((j >= low) & (j < high))
                def _():
                    out[lead + r * capacity : lead + (r + 1) * capacity] = up_grad

        if first is not None:
            for (low, high), out in zip(spans, up_outs):

                @pl.when((j >= low) & (j < high))
                def _():
                    out[:lead] = ins[sources + 3][...]

    ins = list(rows) + [upstream, gate_w, up_w]
    specs = [whole((lines, width))] * sources
    specs += [pl.BlockSpec((slots, step), lambda j, s: (0, j))]
    specs += [pl.BlockSpec((width, step), lambda j, s: (0, j))] * 2
    if first is not None:
        ins.append(first)
        specs.append(pl.BlockSpec((lead, step), lambda j, s: (0, j)))
    return call(
        body,
        "forward_first" if first is None else "forward_rest",
        [expert] + used,
        ins,
        specs,
        [((count, hidden), BF16)] + [((lead + count, size), BF16) for size in up_parts],
        [pl.BlockSpec((count, step), lambda j, s: (0, j))]
        + [
            pl.BlockSpec((lead + count, step), lambda j, s, a=low, b=high: (0, jnp.clip(j - a, 0, b - a - 1)))
            for low, high in spans
        ],
        (hidden // step,),
        scratch=[pltpu.VMEM((count, width), BF16)],
        after=after,
        vmem=60,
    )


def halves_of(width):
    step = 512 if width % 512 == 0 else 128
    steps = width // step
    return step, steps, (steps + 1) // 2


def slot_gradients(places, gate, ups, gate_w, up_w, near=None, after=()):
    width, hidden = gate_w.shape
    count = gate.shape[0]
    skip = 0 if near is None else near.shape[0]
    slots = skip + count
    capacity = slots // len(places) if skip else count // 2
    step, steps, lead = halves_of(width)

    def body(s, ins, outs):
        j = pl.program_id(0)
        wg, wu = ins[0], ins[1]
        across = ((1,), (1,))
        total = dot(ins[2][...], wg[...], across)
        at = 0
        for g in ins[3 : 3 + len(ups)]:
            size = g.shape[1]
            total = total + dot(g[skip:], wu[:, at : at + size], across)
            at += size
        total = total.astype(BF16)
        if near is None:
            outs[0][...] = total
            return

        def put(out):
            for r in range(len(places)):
                at = pl.ds(pl.multiple_of(s[r] * capacity, 16), capacity)
                if r < 2:
                    out[at, :] = ins[-1][r * capacity : (r + 1) * capacity]
                else:
                    out[at, :] = total[(r - 2) * capacity : (r - 1) * capacity]

        @pl.when(j < lead)
        def _():
            put(outs[0])

        @pl.when(j >= lead)
        def _():
            put(outs[1])

    ins = [gate_w, up_w, gate] + list(ups)
    specs = [pl.BlockSpec((step, hidden), lambda j, s: (j, 0))] * 2 + [whole(g.shape) for g in ins[2:]]
    if near is None:
        outs = [((slots, width), BF16)]
        out_specs = [pl.BlockSpec((slots, step), lambda j, s: (0, j))]
    else:
        ins.append(near)
        specs.append(pl.BlockSpec((skip, step), lambda j, s: (0, j)))
        outs = [((slots, lead * step), BF16), ((slots, width - lead * step), BF16)]
        out_specs = [
            pl.BlockSpec((slots, step), lambda j, s: (0, jnp.minimum(j, lead - 1))),
            pl.BlockSpec((slots, step), lambda j, s: (0, jnp.maximum(j - lead, 0))),
        ]
    out = call(
        body,
        "near_gradients" if near is None else "slot_gradients",
        places,
        ins,
        specs,
        outs,
        out_specs,
        (steps,),
        after=after,
        vmem=63,
    )
    return out[0] if near is None else out


def combine(pair, returned, experts, after=()):
    token_count = pair.shape[1]
    slots, width = returned.shape
    capacity = slots // experts
    step = 512 if width % 512 == 0 else 128

    def body(s, ins, refs):
        marks = refs[-1]

        @pl.when(pl.program_id(0) == 0)
        def _():
            earlier = earlier_mask(token_count)
            for r in range(experts):
                marks[r * capacity : (r + 1) * capacity] = slot_marks(ins[0][...], r, capacity, earlier)

        refs[0][...] = dot(marks[...], ins[1][...], ((0,), (0,))).astype(BF16)

    return call(
        body,
        "combine",
        [jnp.int32(0)],
        [pair, returned],
        [whole(pair.shape), pl.BlockSpec((slots, step), lambda j, s: (0, j))],
        [((token_count, width), BF16)],
        [pl.BlockSpec((token_count, step), lambda j, s: (0, j))],
        (width // step,),
        scratch=[pltpu.VMEM((slots, token_count), BF16)],
        after=after,
    )[0]


def pick_rows(expert, blocks, rows, capacity, block, routes=None, after=()):
    sources = len(rows)
    lines = rows[0].shape[0]
    token_count = lines - ROUTE_ROWS
    count = len(blocks)

    def body(s, ins, outs):
        earlier = earlier_mask(token_count)
        picked = []
        for r in range(sources):
            pair = pair_in(ins[r], token_count) if routes is None else ins[sources + r][...]
            pair = pair.astype(F32).astype(jnp.int32)
            mark = slot_marks(pair, s[0], capacity, earlier)
            picked.append(dot(mark, ins[r][:token_count]))
        outs[0][...] = jnp.concatenate(picked, axis=0).astype(BF16).T

    ins, specs = list(rows), []
    for r in range(sources):
        specs.append(pl.BlockSpec((lines, block), lambda j, s: (0, s[1 + j])))
    if routes is not None:
        ins += list(routes)
        specs += [
            pl.BlockSpec((ROUTE_ROWS, token_count), lambda j, s: (token_count // ROUTE_ROWS, 0)) for _ in routes
        ]
    return call(
        body,
        "pick_rows",
        [expert] + list(blocks),
        ins,
        specs,
        [((count * block, sources * capacity), BF16)],
        [pl.BlockSpec((block, sources * capacity), lambda j, s: (j, 0))],
        (count,),
        after=after,
    )[0]


def products(terms, block, part, dtype, name, extras=(), total=None, after=(), vmem=28):
    slots = terms[0][0].shape[1]
    split = 2 if block % 32 == 0 else 1
    lines = block // split

    count = len(terms)
    pieces = sum(len(parts) for _, _, parts in terms)

    def body(s, ins, outs):
        left = jnp.concatenate([p[...] for p in ins[:count]], axis=1)
        right = jnp.concatenate([g[...] for g in ins[count : count + pieces]], axis=0)
        result = dot(left, right)
        if extras:
            result = result + jnp.concatenate([e[...].astype(F32) for e in ins[count + pieces :]], axis=1)
        outs[0][...] = result.astype(dtype)

    ins = [p for p, _, _ in terms]
    specs = [pl.BlockSpec((lines, slots), lambda j, s, i=i: (i * split + j, 0)) for _, i, _ in terms]
    for _, _, parts in terms:
        for array, column in parts:
            ins.append(array)
            specs.append(pl.BlockSpec((array.shape[0], part), lambda j, s, c=column: (0, c)))
    for e in extras:
        ins.append(e)
        specs.append(pl.BlockSpec((lines, e.shape[1]), lambda j, s: (j, 0)))
    return call(
        body,
        name,
        [jnp.int32(0)],
        ins,
        specs,
        [((block, total or part), dtype)],
        [pl.BlockSpec((lines, part), lambda j, s: (j, 0))],
        (split,),
        after=after,
        vmem=vmem,
    )[0]


def finish(own, extra, target, place, total, after=()):
    block, part = own.shape
    ins = [own, extra]
    specs = [whole((block, part))] * 2
    if target is not None:
        ins.append(target)
        specs.append(pl.BlockSpec(memory_space=pl.ANY))

    def body(s, refs, outs):
        outs[0][...] = (refs[0][...] + refs[1][...].astype(F32)).astype(BF16)

    return call(
        body,
        "finish",
        [jnp.int32(0)],
        ins,
        specs,
        [((block, total), BF16)],
        [pl.BlockSpec((block, part), lambda j, s: (0, place))],
        (1,),
        after=after,
        aliases={3: 0} if target is not None else None,
        vmem=60,
    )[0]


def tied(value, *others):
    return lax.optimization_barrier((value,) + others)[0]


def shards(tokens, routes, hidden_grad, w_gate, w_up):
    groups = lax.axis_size("dp")
    experts = lax.axis_size("expert")
    sections = lax.axis_size("section")
    group = lax.axis_index("dp")
    expert = lax.axis_index("expert")
    rows = tokens[0]
    token_count, width = rows.shape
    slots = hidden_grad.shape[3]
    capacity = slots // experts
    hidden = w_gate.shape[3]
    block = width // groups
    gate_w = w_gate[0, 0]
    up_w = w_up[0, 0]
    upstream = hidden_grad[0, 0, 0]
    sets = grouped_pairs(groups)
    up_parts = [hidden // 2, hidden // 2]
    wide = -(-block // 128) * 128
    own_blocks = [group, jnp.where(group < groups // 2, 0, groups - 1)]

    def swap(value):
        return lax.ppermute(value, "expert", [(s, s ^ 1) for s in range(experts)])

    def shift(value, by):
        return lax.ppermute(value, "expert", [(s, (s + 2 * by) % experts) for s in range(experts)])

    def over_groups(value, pairs):
        return lax.ppermute(value, "dp", pairs)

    def to_sources(value):
        back = lax.all_to_all(
            value.reshape(experts, capacity, value.shape[1]), "expert", split_axis=0, concat_axis=0, tiled=True
        )
        return back.reshape(value.shape)

    def passed_on(value):
        return lax.ppermute(value, "section", [(s, (s - 1) % sections) for s in range(sections)])

    def to_ends(value):
        return lax.ppermute(value, "dp", [(1, 0), (groups - 2, groups - 1)])

    chips = range(1, experts // 2)
    places = [jnp.bitwise_xor((expert - 2 * (r // 2)) % experts, r % 2) for r in range(experts)]
    targets = [target_in(pairs, group) for pairs in sets]
    order = list(range(2, len(sets))) + [0, 1]

    pair = routes[0].T
    own, *cut = cut_columns(rows, pair, group, targets, groups, block)
    far_even = [shift(own, by) for by in chips]
    others = {k: over_groups(cut[k], sets[k]) for k in order}
    partner = swap(own)
    near_gate, near_up = forward(expert, places, [own, partner], upstream, gate_w, up_w, [hidden])
    near_back = slot_gradients(places, near_gate, [near_up], gate_w, up_w, after=[near_gate])
    epoch = [others[k] for k in order] + far_even + [near_back]

    near_sent = {k: over_groups(tied(near_gate, *epoch), sets[k]) for k in order}
    far = []
    for value in far_even:
        far += [value, swap(tied(value, *epoch))]
    end_columns = join_columns([(others[k], wide, wide) for k in range(1, len(sets))], after=epoch[:-1])
    end_far = [shift(end_columns, by) for by in chips]
    far_gate, *ups = forward(
        expert, places, far, upstream, gate_w, up_w, up_parts, first=near_up, after=[end_columns]
    )
    own_columns = [own, partner] + far
    own_lines = own_columns
    if wide != block:
        own_columns = [cut_padded(v, own_blocks, block, wide) for v in own_columns]
        own_blocks = [jnp.int32(0), jnp.int32(1)]
    own_picked = pick_rows(
        expert, own_blocks, own_columns, capacity, wide, routes=own_lines, after=[far_gate]
    )
    own_part = join_columns([(others[k], 0, wide) for k in range(len(sets))], after=[own_picked])
    epoch = [near_sent[k] for k in order] + [own_part]

    far_sent = {k: over_groups(tied(far_gate, *epoch), sets[k]) for k in order}
    first_back, second_back = slot_gradients(
        places, far_gate, ups, gate_w, up_w, near=near_back, after=epoch
    )
    first_back = to_sources(first_back)
    end_rows = []
    for value in [end_columns] + end_far:
        end_rows += [value, swap(tied(value, *epoch))]
    column_far = [shift(tied(own_part, *epoch), by) for by in chips]
    end_picked = pick_rows(
        expert, [jnp.int32(k) for k in range(len(sets) - 1)], end_rows, capacity, wide, after=[second_back]
    )
    epoch = [far_sent[k] for k in order] + [end_picked]

    def parts_of(c):
        if c == 0:
            out = [[(near_gate, c), (far_gate, c)]]
            out += [[(near_sent[k], c), (far_sent[k], c)] for k in range(len(sets))]
        else:
            out = [[(ups[c - 1], 0)]] + [[(up_sent[c - 1][k], 0)] for k in range(len(sets))]
        return out

    def for_end(c, after):
        parts = parts_of(c)
        part = up_parts[c - 1] if c else hidden
        terms = [(own_picked, 1, parts[0])]
        terms += [(end_picked, k - 1, parts[1 + k]) for k in reversed(range(1, len(sets)))]
        return products(terms, wide, part, BF16, "for_end", after=after, vmem=60)

    def for_own(c, part, dtype, after, extras=(), total=None):
        parts = parts_of(c)
        terms = [(own_picked, 0, parts[0])]
        terms += [(picked, k, parts[1 + k]) for k in reversed(range(len(sets)))]
        return products(terms, wide, part, dtype, "for_own", extras=extras, total=total, after=after, vmem=60)

    up_sent = []

    def send_up(c):
        up_sent.append({k: over_groups(tied(ups[c], *epoch), sets[k]) for k in order})
        return [up_sent[c][k] for k in order]

    arriving = send_up(0)
    column_rows = []
    for value in [own_part] + column_far:
        column_rows += [value, swap(tied(value, *epoch))]
    end0 = for_end(0, epoch)
    extra0 = to_ends(end0)
    picked = pick_rows(
        expert, [jnp.int32(k) for k in range(len(sets))], column_rows, capacity, wide, after=[end0]
    )
    epoch = arriving + [picked, first_back]

    arriving = send_up(1)
    second_back = to_sources(tied(second_back, *epoch))
    end1 = for_end(1, epoch)
    extra1 = to_ends(end1)
    first_tok = combine(pair, first_back, experts, after=[end1])
    first_passed = passed_on(first_tok)
    gate = for_own(0, hidden, BF16, [first_tok], extras=[extra0])
    epoch = arriving + [gate]

    end2 = for_end(2, epoch)
    extra2 = to_ends(end2)
    second_tok = combine(pair, second_back, experts, after=[end2])
    second_passed = passed_on(second_tok)
    up0 = for_own(1, up_parts[0], BF16, [second_tok], extras=[extra1], total=hidden)
    own2 = for_own(2, up_parts[1], F32, [up0])
    passed = jnp.concatenate([tied(first_passed, own2), second_passed], axis=1)
    up1 = finish(own2, extra2, up0, up_parts[0] // up_parts[1], hidden)
    return (passed[None], gate[None, None, :block], up1[None, None, :block])


def solution(mesh):
    placed = (
        P("section", ("dp", "expert"), None),
        P("section", ("dp", "expert"), None),
        P("section", "dp", "expert", None, None),
        P("section", "expert", None, None),
        P("section", "expert", None, None),
    )
    return jax.shard_map(
        shards,
        mesh=mesh,
        in_specs=placed,
        out_specs=(
            P("section", ("dp", "expert"), None),
            P("section", "expert", "dp", None),
            P("section", "expert", "dp", None),
        ),
        check_vma=False,
    )
```
